256 devices in a mesh: section: 8 (over z), expert: 16 (over y, x), dp: 2 (over core).
Axes of the slice: x: 4, y: 4, z: 8, core: 2. Of those that a mesh axis runs over, the one named last changes fastest.
Arguments:
- stream_up: bfloat16 [8, 2048, 3584], P('section', 'expert', 'dp'), may hold values from -6 to 6
- routes_up: int32 [8, 1, 2048, 1], P('section', None, 'expert'), may hold values from 0 to 3; in each aligned block of 128 rows (0 to 127, 128 to 255, ..., all dimensions but the last counted through in order) at most 40 rows name the same one
- cotangent_down: bfloat16 [8, 2048, 3584], P('section', 'expert', 'dp'), may hold values from -6 to 6
- saved_down: bfloat16 [8, 1, 2048, 3584], P('section', None, 'expert', 'dp'), may hold values from -6 to 6
- routes_down: int32 [8, 1, 2048, 1], P('section', None, 'expert'), may hold values from 0 to 3; in each aligned block of 128 rows (0 to 127, 128 to 255, ..., all dimensions but the last counted through in order) at most 40 rows name the same one
- weight_up: bfloat16 [8, 16, 3584, 256], P('section', 'expert', 'dp'), may hold values from -0.09375 to 0.09375
- weight_down: bfloat16 [8, 16, 256, 3584], P('section', 'expert', None, 'dp'), may hold values from -0.1875 to 0.1875
Outputs:
- stream_out: bfloat16 [8, 2048, 3584], P('section', 'expert', 'dp')
- grad_out: bfloat16 [8, 2048, 3584], P('section', 'expert', 'dp')
The draws below stay inside these ranges and needn't reach their ends.
Inputs may be any that keep to these rules, and one draw needn't show every extreme that they name: `routes_up`: in each aligned block of 128 tokens (the rows of one device) no expert is named by more than 40 tokens, a bound that some block reaches. `routes_down`: in each aligned block of 128 tokens (the rows of one device) no expert is named by more than 40 tokens, a bound that some block reaches.
All inputs are finite; a program needn't handle non-finite values.
Results may differ from the reference program's by a relative error of at most 0.014.
Values may be sent and summed in bfloat16 or wider, within the bound.
No kernel may reach another device: no remote copies, remote signals or barrier semaphores. Data moves between devices by JAX's collectives and lax.ppermute only.
A program may use at most 64 MiB of HBM per device.

```python
import math
import jax
import jax.numpy as jnp
import numpy as np
from jax import lax

D = 3584
HID = 1024
TOK_DEV = 128
TICKS = 1
SPLIT = 4
EXPERTS = 4
HPART = 256
SECTIONS = 8
CAP = 40
TOKENS = 2048
QW = 1792
N_EXPERT = 16
N_DP = 2


def block_scale(rng, shape, shards, least, top_value):
    level = 1.0
    for dim, blocks in shards:
        steps = jax.random.uniform(jax.random.fold_in(jax.random.fold_in(rng, 6), dim), (blocks,), jnp.float32, least / len(shards), top_value / len(shards))
        level = level * jnp.repeat(jnp.exp(steps), shape[dim] // blocks).reshape((-1,) + (1,) * (len(shape) - 1 - dim))
    return level


def assign_block(rng, own, number, rows, amount, top, most, skew):
    order = jax.random.permutation(rng, amount)
    packed, ordinary = portions_of(amount, rows * top, most, skew, True), portions_of(amount, rows * top, most, skew, False)
    places = jnp.arange(amount)

    def named(sizes, offset_by):
        used = int((sizes > 0).sum())
        fixed = max(1, used // 4)
        passed = fixed + (places - fixed + offset_by * (used - fixed)) % max(1, amount - fixed)
        return jnp.zeros((amount,), jnp.int32).at[order[jnp.where(places < fixed, places, passed)]].set(jnp.asarray(sizes, jnp.int32))

    sizes = jnp.where(number % 4 == 0, named(packed, number // 4), named(ordinary, number - number // 4 - 1))
    mixed = jax.random.permutation(jax.random.fold_in(own, 3), amount)
    donor, sink = mixed[0:amount // 2 * 2:2], mixed[1:amount // 2 * 2:2]
    slack = jnp.minimum(sizes[donor] - 1, most - sizes[sink]) // 2
    slack = jnp.where((donor == order[0]) | (sink == order[0]) | (sizes[sink] == 0), 0, jnp.maximum(slack, 0))
    passed = jax.random.randint(jax.random.fold_in(own, 4), (amount // 2,), 0, 1 << 20) % (slack + 1)
    sizes = sizes.at[donor].add(-passed).at[sink].add(passed)
    items = jnp.searchsorted(jnp.cumsum(sizes), jnp.arange(rows * top), side="right").astype(jnp.int32)
    grid = items.reshape(top, rows).T
    grid = grid[jax.random.permutation(jax.random.fold_in(own, 1), rows)]
    offset_by = jax.random.randint(jax.random.fold_in(own, 2), (rows, 1), 0, top)
    return jnp.take_along_axis(grid, (jnp.arange(top)[None, :] + offset_by) % top, axis=1)


def portions_of(number_of, total, limit, slope, full):
    loads = [(1 << 20) // math.isqrt(grade ** slope) + 1 for grade in range(1, number_of + 1)]
    largest = limit if full else min(limit, max(-(-total // number_of), total * loads[0] // sum(loads)))
    least = 1 if total - largest >= number_of - 1 else 0
    holding, rest = [largest] + [least] * (number_of - 1), total - largest - least * (number_of - 1)
    while rest > 0:
        free = [i for i in range(1, number_of) if holding[i] < largest] or [i for i in range(1, number_of) if holding[i] < limit]
        whole, left = sum([loads[i] for i in free]), rest
        for i in free:
            more = min(limit - holding[i], max(1, left * loads[i] // whole), rest)
            holding[i] = holding[i] + more
            rest = rest - more
    return np.array(holding)


def gaussian(rng, extent, spread, most, cuts=(), held_as=jnp.bfloat16):
    result = jax.random.normal(rng, extent, jnp.float32) * spread
    if len(cuts) > 0:
        result = block_scale(rng, extent, cuts, -0.22, 0.18) * result
    return jnp.clip(result, min=-most, max=most).astype(held_as)


def setup_inputs(seed: int = 0) -> dict:
    keys = jax.random.split(jax.random.key(seed), 8)
    stream_up = gaussian(keys[0], (SECTIONS, TOKENS, D), 1.0, 6.0, ((0, 8), (1, 16), (2, 2)))
    routes_up_keys = jax.random.split(jax.random.fold_in(keys[1], 1), SECTIONS * TICKS * TOKENS // TOK_DEV)
    routes_up_turns = jax.random.permutation(jax.random.fold_in(keys[1], 3), SECTIONS * TICKS * TOKENS // TOK_DEV)
    routes_up = jax.vmap(lambda own, number: assign_block(jax.random.fold_in(keys[1], 2), own, number, TOK_DEV, EXPERTS, 1, CAP, 2))(routes_up_keys, routes_up_turns).reshape((SECTIONS, TICKS, TOKENS, 1))
    cotangent_down = gaussian(keys[2], (SECTIONS, TOKENS, D), 1.0, 6.0, ((0, 8), (1, 16), (2, 2)))
    saved_down = gaussian(keys[3], (SECTIONS, TICKS, TOKENS, D), 1.0, 6.0, ((0, 8), (2, 16), (3, 2)))
    routes_down_keys = jax.random.split(jax.random.fold_in(keys[4], 1), SECTIONS * TICKS * TOKENS // TOK_DEV)
    routes_down_turns = jax.random.permutation(jax.random.fold_in(keys[4], 3), SECTIONS * TICKS * TOKENS // TOK_DEV)
    routes_down = jax.vmap(lambda own, number: assign_block(jax.random.fold_in(keys[4], 2), own, number, TOK_DEV, EXPERTS, 1, CAP, 2))(routes_down_keys, routes_down_turns).reshape((SECTIONS, TICKS, TOKENS, 1))
    weight_up = gaussian(keys[5], (SECTIONS, N_EXPERT, D, HPART), D ** -0.5, 0.09375, ((0, 8), (1, 16), (2, 2)))
    weight_down = gaussian(keys[6], (SECTIONS, N_EXPERT, HPART, D), HID ** -0.5, 0.1875, ((0, 8), (1, 16), (3, 2)))
    return dict(stream_up=stream_up, routes_up=routes_up, cotangent_down=cotangent_down, saved_down=saved_down, routes_down=routes_down, weight_up=weight_up, weight_down=weight_down)


def silu_grad(values):
    sigma = jax.nn.sigmoid(values)
    return sigma * (1.0 + values * (1.0 - sigma))

def assign_slots(expert_ids):
    groups = expert_ids.reshape(N_EXPERT, TOK_DEV)
    onehot = (groups[:, :, None] == jnp.arange(EXPERTS, dtype=jnp.int32)[None, None, :]).astype(jnp.int32)
    before = jnp.cumsum(onehot, axis=1) - onehot
    position = lax.optimization_barrier(jnp.sum(before * onehot, axis=2))
    slot_index = jnp.arange(N_EXPERT, dtype=jnp.int32)[:, None] * CAP + position
    return slot_index.reshape(-1).astype(jnp.int32)

def dispatch(row_data, expert_ids, slot_index):
    buffer = jnp.zeros((EXPERTS, N_EXPERT * CAP, D), row_data.dtype)
    return buffer.at[expert_ids, slot_index].set(row_data)

def expand_up(up_blocks):
    return up_blocks.reshape(EXPERTS, SPLIT, D, HPART).transpose(0, 2, 1, 3).reshape(EXPERTS, D, HID)

def expand_down(down_blocks):
    return down_blocks.reshape(EXPERTS, HID, D)

def split_sum(left, right):
    row_total = left.shape[1]
    left_blocks = left.reshape(EXPERTS, row_total, N_DP, QW).astype(jnp.float32)
    right_blocks = right.reshape(EXPERTS, N_DP, QW, HID).astype(jnp.float32)
    partial_value = jnp.einsum('esqd,eqdh->eqsh', left_blocks, right_blocks)
    rounded = lax.optimization_barrier(partial_value.astype(jnp.bfloat16))
    return lax.optimization_barrier(jnp.sum(rounded.astype(jnp.float32), axis=1))

def block_sum(left, right):
    row_total = left.shape[1]
    left_blocks = left.reshape(EXPERTS, row_total, SPLIT, HPART).astype(jnp.float32)
    right_blocks = right.reshape(EXPERTS, SPLIT, HPART, D).astype(jnp.float32)
    partial_value = jnp.einsum('esjh,ejhd->ejsd', left_blocks, right_blocks)
    rounded = lax.optimization_barrier(partial_value.astype(jnp.bfloat16))
    return lax.optimization_barrier(jnp.sum(rounded.astype(jnp.float32), axis=1))

def forward_layer(row_data, expert_ids, up_full, down_full):
    slot_index = assign_slots(expert_ids)
    hidden_in = split_sum(dispatch(row_data, expert_ids, slot_index), up_full)
    activated = jax.nn.silu(hidden_in).astype(jnp.bfloat16)
    expert_out = block_sum(activated, down_full)
    returned = expert_out[expert_ids, slot_index]
    return (row_data.astype(jnp.float32) + returned).astype(jnp.bfloat16)

def backward_layer(saved_rows, cotangent, expert_ids, up_full, down_full):
    slot_index = assign_slots(expert_ids)
    hidden_in = split_sum(dispatch(saved_rows, expert_ids, slot_index), up_full)
    hidden_grad_in = split_sum(dispatch(cotangent, expert_ids, slot_index), jnp.swapaxes(down_full, 1, 2))
    hidden_grad = (hidden_grad_in * silu_grad(hidden_in)).astype(jnp.bfloat16)
    input_grad = block_sum(hidden_grad, jnp.swapaxes(up_full, 1, 2))
    returned = input_grad[expert_ids, slot_index]
    return (cotangent.astype(jnp.float32) + returned).astype(jnp.bfloat16)

def reference(stream_up, routes_up, cotangent_down, saved_down, routes_down, weight_up, weight_down):
    upward = stream_up
    downward = cotangent_down
    for step_index in range(TICKS):
        forward_list = []
        backward_list = []
        for layer_index in range(SECTIONS):
            up_full = expand_up(weight_up[layer_index])
            down_full = expand_down(weight_down[layer_index])
            forward_list.append(forward_layer(upward[layer_index], routes_up[layer_index, step_index, :, 0], up_full, down_full))
            backward_list.append(backward_layer(saved_down[layer_index, step_index], downward[layer_index], routes_down[layer_index, step_index, :, 0], up_full, down_full))
        upward = jnp.roll(jnp.stack(forward_list), 1, axis=0)
        downward = jnp.roll(jnp.stack(backward_list), -1, axis=0)
    return (upward, downward)
```

```python
import functools

import jax
import jax.numpy as jnp
from jax import lax
from jax.experimental import pallas as pl
from jax.experimental.pallas import tpu as pltpu
from jax.sharding import PartitionSpec as P

NX = 4
NY = 4
NZ = 8
CAP = 40
ROWS = 128
BF = jnp.bfloat16
F32 = jnp.float32
VM = pl.BlockSpec(memory_space=pltpu.VMEM)
SM = pl.BlockSpec(memory_space=pltpu.SMEM)
LIMIT = 24 * 1024 * 1024


def move_x(v, d):
    return lax.ppermute(
        v, "expert", [(y * NX + x, y * NX + (x + d) % NX) for y in range(NY) for x in range(NX)]
    )


def move_y(v, d):
    return lax.ppermute(
        v, "expert", [(y * NX + x, (y + d) % NY * NX + x) for y in range(NY) for x in range(NX)]
    )


def move_z(v, d):
    return lax.ppermute(v, "section", [(z, (z + d) % NZ) for z in range(NZ)])


def move_zy(v, dz, dy):
    n = NX * NY
    pairs = [
        (z * n + y * NX + x, (z + dz) % NZ * n + (y + dy) % NY * NX + x)
        for z in range(NZ)
        for y in range(NY)
        for x in range(NX)
    ]
    return lax.ppermute(v, ("section", "expert"), pairs)


def swap(v):
    return lax.ppermute(v, "dp", [(0, 1), (1, 0)])


def call(kernel, outs, flops, nbytes, in_specs, *args):
    return pl.pallas_call(
        kernel,
        out_shape=outs,
        in_specs=in_specs,
        out_specs=jax.tree.map(lambda _: VM, outs),
        compiler_params=pltpu.CompilerParams(vmem_limit_bytes=LIMIT),
        cost_estimate=pl.CostEstimate(flops=flops, bytes_accessed=nbytes, transcendentals=0),
    )(*args)


def sds(shape, dtype=BF):
    return jax.ShapeDtypeStruct(shape, dtype)


def nn(a, b):
    return jnp.dot(a, b, preferred_element_type=F32)


def nt(a, b):
    return lax.dot_general(a, b, (((1,), (1,)), ((), ())), preferred_element_type=F32)


def tn(a, b):
    return lax.dot_general(a, b, (((0,), (0,)), ((), ())), preferred_element_type=F32)


def slot_table(ids, y):
    n = ids.shape[1]
    rel = jnp.bitwise_and(ids - y + NY, NY - 1)
    onehot = (lax.broadcasted_iota(jnp.int32, (8, n), 0) == rel).astype(F32)
    earlier = lax.broadcasted_iota(jnp.int32, (n, n), 0) < lax.broadcasted_iota(
        jnp.int32, (n, n), 1
    )
    before = nn(onehot.astype(BF), earlier.astype(F32).astype(BF))
    rank = jnp.sum(before * onehot, axis=0, keepdims=True).astype(jnp.int32)
    slot = rel * CAP + rank
    table = lax.broadcasted_iota(jnp.int32, (NY * CAP, n), 0) == slot
    return table.astype(F32).astype(BF)


def columns(width, step=256):
    return [slice(c, c + step) for c in range(0, width, step)]


def dispatch_kernel(y_ref, up_ref, down_ref, fwd_ref, saved_ref, grad_ref, *outs):
    y = y_ref[0]
    table_up = slot_table(up_ref[...], y)
    table_down = slot_table(down_ref[...], y)
    for c in columns(fwd_ref.shape[1]):
        f = nn(table_up, fwd_ref[:, c])
        s = nn(table_down, saved_ref[:, c])
        g = nn(table_down, grad_ref[:, c])
        pad = jnp.zeros((ROWS - 3 * CAP, f.shape[1]), F32)
        for rel in range(NY):
            r = slice(rel * CAP, (rel + 1) * CAP)
            outs[rel][:, c] = jnp.concatenate([f[r], s[r], g[r], pad], axis=0).astype(BF)


def up_kernel(r0, r1, r2, r3, *refs):
    *weights, out = refs
    rows = jnp.concatenate([r[0 : 2 * CAP, :] for r in (r0, r1, r2, r3)], axis=0)
    for i, w in enumerate(weights):
        out[:, i * 256 : (i + 1) * 256] = nn(rows, w[...]).astype(BF)


def up_halves_kernel(r0, r1, r2, r3, wa, wb, out):
    rows = jnp.concatenate([r[0 : 2 * CAP, :] for r in (r0, r1, r2, r3)], axis=0)
    half = wa.shape[0]
    out[...] = (nn(rows[:, :half], wa[...]) + nn(rows[:, half:], wb[...])).astype(BF)


def down_kernel(r0, r1, r2, r3, *refs):
    *weights, out = refs
    rows = jnp.concatenate([r[2 * CAP : ROWS, :] for r in (r0, r1, r2, r3)], axis=0)
    at = 0
    for w in weights:
        n = w.shape[0]
        out[:, at : at + n] = nt(rows, w[...]).astype(BF)
        at += n


def pick(v, start, stride):
    return jnp.concatenate(
        [v[i * stride + start : i * stride + start + CAP, :] for i in range(NY)], axis=0
    )


def added(a_ref, b_ref):
    return a_ref[...].astype(F32) + b_ref[...].astype(F32)


def activate(pu):
    v = pick(pu, 0, 2 * CAP)
    return (v * jax.nn.sigmoid(v)).astype(BF)


def grad_hidden(pu, pv):
    v = pick(pu, CAP, 2 * CAP)
    g = pick(pv, 0, ROWS - 2 * CAP)
    q = jax.nn.sigmoid(v)
    return (g * (q * (1.0 + v * (1.0 - q)))).astype(BF)


def mid_kernel(pu, qu, pv, qv, u0, u1, u2, v0, v1, v2, acc_f, acc_b):
    su = added(pu, qu)
    act = activate(su)
    hid = grad_hidden(su, added(pv, qv))
    for c in columns(acc_f.shape[1]):
        acc_f[:, c] = sum(
            nn(act[:, i * 256 : (i + 1) * 256], v[:, c]) for i, v in enumerate((v0, v1, v2))
        )
        acc_b[:, c] = sum(
            nt(hid[:, i * 256 : (i + 1) * 256], u[c, :]) for i, u in enumerate((u0, u1, u2))
        )


def last_f_kernel(pu, qu, va, vb, acc, *outs):
    act = activate(added(pu, qu))
    half = va.shape[0]
    for c in columns(acc.shape[1]):
        t = acc[:, c] + nn(act[:, :half], va[:, c]) + nn(act[:, half:], vb[:, c])
        for i in range(NY):
            outs[i][:, c] = t[i * CAP : (i + 1) * CAP].astype(BF)


def last_b_kernel(pu, qu, pv, qv, ua, ub, acc, *outs):
    hid = grad_hidden(added(pu, qu), added(pv, qv))
    half = ua.shape[0]
    for u, base in ((ua, 0), (ub, half)):
        for c in columns(half, 128):
            o = slice(base + c.start, base + c.stop)
            t = acc[:, o] + nt(hid, u[c, :])
            for i in range(NY):
                outs[i][:, o] = t[i * CAP : (i + 1) * CAP].astype(BF)


def combine_kernel(y_ref, ids_ref, rows_ref, f0, f1, f2, f3, out):
    table = slot_table(ids_ref[...], y_ref[0])
    for c in columns(rows_ref.shape[1]):
        got = jnp.concatenate([f[:, c].astype(F32) for f in (f0, f1, f2, f3)], axis=0).astype(BF)
        out[:, c] = (rows_ref[:, c].astype(F32) + tn(table, got)).astype(BF)


def per_device(
    stream_up, routes_up, cotangent_down, saved_down, routes_down, weight_up, weight_down
):
    u_own = weight_up[0, 0]
    v_own = weight_down[0, 0]
    fwd = stream_up[0]
    cot = cotangent_down[0]
    saved = saved_down[0, 0]
    n, width = fwd.shape
    hp = u_own.shape[1]
    ids_up = routes_up.reshape(1, n)
    ids_down = routes_down.reshape(1, n)
    y = (lax.axis_index("expert") // NX).reshape(1)

    u_l, u_r = move_x(u_own, 1), move_x(u_own, -1)
    v_l, v_r = move_x(v_own, 1), move_x(v_own, -1)

    sent = call(
        dispatch_kernel,
        [sds((ROWS, width))] * NY,
        6 * 160 * 128 * width,
        7 * 128 * width * 2,
        [SM] + [VM] * 5,
        y,
        ids_up,
        ids_down,
        fwd,
        saved,
        cot,
    )
    rows = [sent[0]] + [move_y(sent[d], d) for d in range(1, NY)]

    fwd_next, ids_up_next = move_z(fwd, 1), move_z(ids_up, 1)
    cot_next, ids_down_next = move_z(cot, -1), move_z(ids_down, -1)

    u_a, u_b = move_x(u_l[: width // 2], 1), move_x(u_r[width // 2 :], -1)
    v_a, v_b = move_x(v_l[: hp // 2], 1), move_x(v_r[hp // 2 :], -1)

    mm = 2 * 320 * width * hp
    pu = call(
        up_kernel, sds((2 * CAP * NY, 3 * hp)), 3 * mm, 4 << 20, [VM] * 7, *rows, u_own, u_l, u_r
    )
    qu = swap(pu)
    pv = call(
        down_kernel,
        sds(((ROWS - 2 * CAP) * NY, 3 * hp)),
        2 * mm,
        4 << 20,
        [VM] * 7,
        *rows,
        v_own,
        v_l,
        v_r,
    )
    qv = swap(pv)
    acc_f, acc_b = call(
        mid_kernel,
        [sds((NY * CAP, width), F32)] * 2,
        3 * mm,
        8 << 20,
        [VM] * 10,
        pu,
        qu,
        pv,
        qv,
        u_own,
        u_l,
        u_r,
        v_own,
        v_l,
        v_r,
    )
    pu2 = call(up_halves_kernel, sds((2 * CAP * NY, hp)), mm, 2 << 20, [VM] * 6, *rows, u_a, u_b)
    qu2 = swap(pu2)
    pv2 = call(
        down_kernel,
        sds(((ROWS - 2 * CAP) * NY, hp)),
        mm // 2,
        2 << 20,
        [VM] * 6,
        *rows,
        v_a,
        v_b,
    )
    qv2 = swap(pv2)
    outs = [sds((CAP, width))] * NY
    res_f = call(
        last_f_kernel, outs, mm // 2, 2 << 20, [VM] * 5, pu2, qu2, v_a, v_b, acc_f
    )
    res_b = call(
        last_b_kernel, outs, mm // 2, 2 << 20, [VM] * 7, pu2, qu2, pv2, qv2, u_a, u_b, acc_b
    )
    got_f = [move_zy(r, 1, -d) for d, r in enumerate(res_f)]
    got_b = [move_zy(r, -1, -d) for d, r in enumerate(res_b)]
    final = functools.partial(
        call,
        combine_kernel,
        sds((n, width)),
        2 * 160 * 128 * width,
        2 << 20,
        [SM] + [VM] * 6,
        y,
    )
    out_f = final(ids_up_next, fwd_next, *got_f)
    out_b = final(ids_down_next, cot_next, *got_b)
    return (out_f[None], out_b[None])


def solution(mesh):
    return jax.shard_map(
        per_device,
        mesh=mesh,
        in_specs=(
            P("section", "expert", "dp"),
            P("section", None, "expert", None),
            P("section", "expert", "dp"),
            P("section", None, "expert", "dp"),
            P("section", None, "expert", None),
            P("section", "expert", "dp", None),
            P("section", "expert", None, "dp"),
        ),
        out_specs=(P("section", "expert", "dp"), P("section", "expert", "dp")),
        check_vma=False,
    )
```

```python
import functools

import jax
import jax.numpy as jnp
from jax import lax
from jax.experimental import pallas as pl
from jax.experimental.pallas import tpu as pltpu
from jax.sharding import PartitionSpec as P

NX = 4
NY = 4
NZ = 8
CAP = 40
ROWS = 128
BF = jnp.bfloat16
F32 = jnp.float32
VM = pl.BlockSpec(memory_space=pltpu.VMEM)
ANY = pl.BlockSpec(memory_space=pl.ANY)
HBM = pl.BlockSpec(memory_space=pltpu.HBM)
SM = pl.BlockSpec(memory_space=pltpu.SMEM)

CU = 8 * 10**9
LIMIT = 24 * 1024 * 1024


def move_x(v, d):
    return lax.ppermute(
        v, "expert", [(y * NX + x, y * NX + (x + d) % NX) for y in range(NY) for x in range(NX)]
    )


def move_y(v, d):
    return lax.ppermute(
        v, "expert", [(y * NX + x, (y + d) % NY * NX + x) for y in range(NY) for x in range(NX)]
    )


def move_z(v, d):
    return lax.ppermute(v, "section", [(z, (z + d) % NZ) for z in range(NZ)])


def move_zy(v, dz, dy):
    n = NX * NY
    pairs = [
        (z * n + y * NX + x, (z + dz) % NZ * n + (y + dy) % NY * NX + x)
        for z in range(NZ)
        for y in range(NY)
        for x in range(NX)
    ]
    return lax.ppermute(v, ("section", "expert"), pairs)


def swap(v):
    return lax.ppermute(v, "dp", [(0, 1), (1, 0)])


def call(kernel, outs, flops, nbytes, in_specs, *args, scratch=()):
    return pl.pallas_call(
        kernel,
        out_shape=outs,
        scratch_shapes=scratch,
        in_specs=in_specs,
        out_specs=jax.tree.map(lambda _: VM, outs),
        compiler_params=pltpu.CompilerParams(vmem_limit_bytes=LIMIT),
        cost_estimate=pl.CostEstimate(flops=flops, bytes_accessed=nbytes, transcendentals=0),
    )(*args)


def sds(shape, dtype=BF):
    return jax.ShapeDtypeStruct(shape, dtype)


def nn(a, b):
    return jnp.dot(a, b, preferred_element_type=F32)


def nt(a, b):
    return lax.dot_general(a, b, (((1,), (1,)), ((), ())), preferred_element_type=F32)


def tn(a, b):
    return lax.dot_general(a, b, (((0,), (0,)), ((), ())), preferred_element_type=F32)


def slot_table(ids, y):
    n = ids.shape[1]
    rel = jnp.bitwise_and(ids - y + NY, NY - 1)
    onehot = (lax.broadcasted_iota(jnp.int32, (8, n), 0) == rel).astype(F32)
    earlier = lax.broadcasted_iota(jnp.int32, (n, n), 0) < lax.broadcasted_iota(
        jnp.int32, (n, n), 1
    )
    before = nn(onehot.astype(BF), earlier.astype(F32).astype(BF))
    rank = jnp.sum(before * onehot, axis=0, keepdims=True).astype(jnp.int32)
    slot = rel * CAP + rank
    table = lax.broadcasted_iota(jnp.int32, (NY * CAP, n), 0) == slot
    return table.astype(F32).astype(BF)


def columns(width, step=256):
    return [slice(c, c + step) for c in range(0, width, step)]


def dispatch_kernel(y_ref, *refs):
    ins, outs, scratch, sems = refs[:5], refs[5:9], refs[9:14], refs[14]
    copies = [pltpu.make_async_copy(i, s, sems.at[k]) for k, (i, s) in enumerate(zip(ins, scratch))]
    for c in copies:
        c.start()
    up, down, fwd, saved, grad = scratch
    y = y_ref[0]
    copies[0].wait()
    copies[1].wait()
    table_up = slot_table(up[...], y)
    table_down = slot_table(down[...], y)
    for c in copies[2:]:
        c.wait()
    for c in columns(fwd.shape[1]):
        f = nn(table_up, fwd[:, c])
        s = nn(table_down, saved[:, c])
        g = nn(table_down, grad[:, c])
        pad = jnp.zeros((ROWS - 3 * CAP, f.shape[1]), F32)
        for rel in range(NY):
            r = slice(rel * CAP, (rel + 1) * CAP)
            outs[rel][:, c] = jnp.concatenate([f[r], s[r], g[r], pad], axis=0).astype(BF)


def table_kernel(y_ref, ids_f, ids_b, out_f, out_b):
    out_f[...] = slot_table(ids_f[...], y_ref[0])
    out_b[...] = slot_table(ids_b[...], y_ref[0])


def held_kernel(v_ref, *refs):
    out, sem = refs[-2:]
    c = pltpu.make_async_copy(v_ref, out, sem)
    c.start()
    c.wait()


def parts_kernel(left, right, out_a, out_b):
    half = out_a.shape[0]
    out_a[...] = left[:half, :]
    out_b[...] = right[half:, :]


def up_kernel(r0, r1, r2, r3, token, *refs):
    *weights, out = refs
    rows = jnp.concatenate([r[0 : 2 * CAP, :] for r in (r0, r1, r2, r3)], axis=0)
    for i, w in enumerate(weights):
        out[:, i * 256 : (i + 1) * 256] = nn(rows, w[...]).astype(BF)


def up_halves_kernel(r0, r1, r2, r3, wa, wb, out):
    rows = jnp.concatenate([r[0 : 2 * CAP, :] for r in (r0, r1, r2, r3)], axis=0)
    half = wa.shape[0]
    out[...] = (nn(rows[:, :half], wa[...]) + nn(rows[:, half:], wb[...])).astype(BF)


def down_kernel(r0, r1, r2, r3, token, *refs):
    *weights, out = refs
    rows = jnp.concatenate([r[2 * CAP : ROWS, :] for r in (r0, r1, r2, r3)], axis=0)
    at = 0
    for w in weights:
        n = w.shape[0]
        out[:, at : at + n] = nt(rows, w[...]).astype(BF)
        at += n


def pick(v, start, stride):
    return jnp.concatenate(
        [v[i * stride + start : i * stride + start + CAP, :] for i in range(NY)], axis=0
    )


def added(a, b):
    return a.astype(F32) + b.astype(F32)


def activate(pu):
    v = pick(pu, 0, 2 * CAP)
    return (v * jax.nn.sigmoid(v)).astype(BF)


def grad_hidden(pu, pv):
    v = pick(pu, CAP, 2 * CAP)
    g = pick(pv, 0, ROWS - 2 * CAP)
    q = jax.nn.sigmoid(v)
    return (g * (q * (1.0 + v * (1.0 - q)))).astype(BF)


def mid_kernel(r0, r1, r2, r3, pu, qu, pv, qv, u0, u1, u2, v0, v1, v2, acc_f, acc_b):
    su = added(pu[...], qu[...])
    act = activate(su)
    hid = grad_hidden(su, added(pv[...], qv[...]))
    for c in columns(acc_f.shape[1]):
        rows = [r[:, c].astype(F32) for r in (r0, r1, r2, r3)]
        f = jnp.concatenate([r[:CAP] for r in rows], axis=0)
        b = jnp.concatenate([r[2 * CAP : 3 * CAP] for r in rows], axis=0)
        for i, (u, v) in enumerate(((u0, v0), (u1, v1), (u2, v2))):
            f += nn(act[:, i * 256 : (i + 1) * 256], v[:, c])
            b += nt(hid[:, i * 256 : (i + 1) * 256], u[c, :])
        acc_f[:, c] = f
        acc_b[:, c] = b


def last_f_kernel(pu, qu, va, vb, acc, token, *outs):
    act = activate(added(pu[...], qu[...]))
    half = va.shape[0]
    for c in columns(acc.shape[1]):
        t = acc[:, c] + nn(act[:, :half], va[:, c]) + nn(act[:, half:], vb[:, c])
        for i, o in enumerate(outs):
            o[:, c] = t[i * CAP : (i + 1) * CAP].astype(BF)


def last_b_kernel(pu, qu, pv, qv, ua, ub, acc, token, *outs):
    hid = grad_hidden(added(pu[...], qu[...]), added(pv[...], qv[...]))
    half = ua.shape[0]
    for u, base in ((ua, 0), (ub, half)):
        for c in columns(half, 128):
            o = slice(base + c.start, base + c.stop)
            t = acc[:, o] + nt(hid, u[c, :])
            for i, out in enumerate(outs):
                out[:, o] = t[i * CAP : (i + 1) * CAP].astype(BF)


def combine_kernel(table, f0, f1, f2, f3, out):
    for c in columns(out.shape[1]):
        got = jnp.concatenate([f[:, c].astype(F32) for f in (f0, f1, f2, f3)], axis=0).astype(BF)
        out[:, c] = tn(table[...], got).astype(BF)


def per_device(
    stream_up, routes_up, cotangent_down, saved_down, routes_down, weight_up, weight_down
):
    u_own = weight_up[0, 0]
    v_own = weight_down[0, 0]
    fwd = stream_up[0]
    cot = cotangent_down[0]
    saved = saved_down[0, 0]
    n, width = fwd.shape
    hp = u_own.shape[1]
    ids_up = routes_up.reshape(1, n)
    ids_down = routes_down.reshape(1, n)
    y = (lax.axis_index("expert") // NX).reshape(1)
    mm = 2 * 320 * width * hp

    def parts(left, right, cost):
        half = sds((left.shape[0] // 2, left.shape[1]))
        return call(
            parts_kernel, [half] * 2, cost, 4 * half.shape[0] * half.shape[1], [VM] * 2, left, right
        )

    u_l, u_r = move_x(u_own, 1), move_x(u_own, -1)
    v_l, v_r = move_x(v_own, 1), move_x(v_own, -1)
    to_r, to_l = parts(u_l, u_r, CU)
    to_u = to_r
    u_a, u_b = move_x(to_r, 1), move_x(to_l, -1)
    to_r, to_l = parts(v_l, v_r, 0)
    to_v = to_r
    v_a, v_b = move_x(to_r, 1), move_x(to_l, -1)

    ids_f, ids_b = move_z(ids_up, 1), move_z(ids_down, -1)
    table_f, table_b = call(
        table_kernel, [sds((NY * CAP, n))] * 2, 0, 4 * NY * CAP * n, [SM, VM, VM], y, ids_f, ids_b
    )

    def held(v, cost, *tokens):
        return call(
            held_kernel,
            sds(v.shape),
            cost,
            4 * ROWS * width,
            [ANY] * (1 + len(tokens)),
            v,
            *tokens,
            scratch=[pltpu.SemaphoreType.DMA],
        )

    sent = call(
        dispatch_kernel,
        [sds((ROWS, width))] * NY,
        6 * 160 * 128 * width,
        7 * 128 * width * 2,
        [SM] + [ANY] * 5,
        y,
        ids_up,
        ids_down,
        fwd,
        saved,
        cot,
        scratch=[pltpu.VMEM((1, n), jnp.int32)] * 2
        + [pltpu.VMEM((n, width), BF)] * 3
        + [pltpu.SemaphoreType.DMA((5,))],
    )
    row2 = move_y(sent[2], 2)
    row1 = move_y(held(sent[1], 0, row2, table_f), 1)
    row3 = move_y(held(sent[3], 0, row1, to_u), 3)
    rows = [sent[0], row1, row2, row3]

    pu = call(
        up_kernel,
        sds((2 * CAP * NY, 3 * hp)),
        3 * mm,
        4 << 20,
        [VM] * 4 + [ANY] + [VM] * 3,
        *rows,
        to_v,
        u_own,
        u_l,
        u_r,
    )
    qu = swap(pu)
    pv = call(
        down_kernel,
        sds(((ROWS - 2 * CAP) * NY, 3 * hp)),
        2 * mm,
        4 << 20,
        [VM] * 4 + [ANY] + [VM] * 3,
        *rows,
        pu,
        v_own,
        v_l,
        v_r,
    )
    qv = swap(pv)
    acc_f, acc_b = call(
        mid_kernel,
        [sds((NY * CAP, width), F32)] * 2,
        3 * mm,
        8 << 20,
        [VM] * 14,
        *rows,
        pu,
        qu,
        pv,
        qv,
        u_own,
        u_l,
        u_r,
        v_own,
        v_l,
        v_r,
    )
    pu2 = call(up_halves_kernel, sds((2 * CAP * NY, hp)), mm, 2 << 20, [VM] * 6, *rows, u_a, u_b)
    qu2 = swap(pu2)
    pv2 = call(
        down_kernel,
        sds(((ROWS - 2 * CAP) * NY, hp)),
        mm // 2,
        2 << 20,
        [VM] * 4 + [ANY] + [VM] * 2,
        *rows,
        acc_b,
        v_a,
        v_b,
    )
    qv2 = swap(pv2)
    outs = [sds((CAP, width))] * NY
    res_f = call(
        last_f_kernel,
        outs,
        mm // 2,
        2 << 20,
        [VM] * 5 + [ANY],
        pu2,
        qu2,
        v_a,
        v_b,
        acc_f,
        pv2,
    )
    got_f = [move_zy(r, 1, -d) for d, r in enumerate(res_f)]
    res_b = call(
        last_b_kernel,
        outs,
        mm // 2,
        2 << 20,
        [VM] * 7 + [ANY],
        pu2,
        qu2,
        pv2,
        qv2,
        u_a,
        u_b,
        acc_b,
        res_f[2],
    )
    got_b = [move_zy(r, -1, -d) for d, r in enumerate(res_b)]
    final = functools.partial(
        call, combine_kernel, sds((n, width)), 2 * 160 * 128 * width, 2 << 20, [VM] * 5
    )
    out_f = final(table_f, *got_f)
    out_b = final(table_b, *got_b)
    return (out_f[None], out_b[None])


def solution(mesh):
    return jax.shard_map(
        per_device,
        mesh=mesh,
        in_specs=(
            P("section", "expert", "dp"),
            P("section", None, "expert", None),
            P("section", "expert", "dp"),
            P("section", None, "expert", "dp"),
            P("section", None, "expert", None),
            P("section", "expert", "dp", None),
            P("section", "expert", None, "dp"),
        ),
        out_specs=(P("section", "expert", "dp"), P("section", "expert", "dp")),
        check_vma=False,
    )
```

```python
import functools

import jax
import jax.numpy as jnp
from jax import lax
from jax.experimental import pallas as pl
from jax.experimental.pallas import tpu as pltpu
from jax.sharding import PartitionSpec as P

NX = 4
NY = 4
NZ = 8
CAP = 40
ROWS = 128
BF = jnp.bfloat16
F32 = jnp.float32
VM = pl.BlockSpec(memory_space=pltpu.VMEM)
ANY = pl.BlockSpec(memory_space=pl.ANY)
HBM = pl.BlockSpec(memory_space=pltpu.HBM)
SM = pl.BlockSpec(memory_space=pltpu.SMEM)

CU = 8 * 10**9
CU2 = 6 * 10**9
LIMIT = 24 * 1024 * 1024


def move_x(v, d):
    return lax.ppermute(
        v, "expert", [(y * NX + x, y * NX + (x + d) % NX) for y in range(NY) for x in range(NX)]
    )


def move_y(v, d):
    return lax.ppermute(
        v, "expert", [(y * NX + x, (y + d) % NY * NX + x) for y in range(NY) for x in range(NX)]
    )


def move_z(v, d):
    return lax.ppermute(v, "section", [(z, (z + d) % NZ) for z in range(NZ)])


def move_zy(v, dz, dy):
    n = NX * NY
    pairs = [
        (z * n + y * NX + x, (z + dz) % NZ * n + (y + dy) % NY * NX + x)
        for z in range(NZ)
        for y in range(NY)
        for x in range(NX)
    ]
    return lax.ppermute(v, ("section", "expert"), pairs)


def swap(v):
    return lax.ppermute(v, "dp", [(0, 1), (1, 0)])


def call(kernel, outs, flops, nbytes, in_specs, *args, scratch=(), out_specs=None):
    return pl.pallas_call(
        kernel,
        out_shape=outs,
        scratch_shapes=scratch,
        in_specs=in_specs,
        out_specs=out_specs or jax.tree.map(lambda _: VM, outs),
        compiler_params=pltpu.CompilerParams(vmem_limit_bytes=LIMIT),
        cost_estimate=pl.CostEstimate(flops=flops, bytes_accessed=nbytes, transcendentals=0),
    )(*args)


def sds(shape, dtype=BF):
    return jax.ShapeDtypeStruct(shape, dtype)


def nn(a, b):
    return jnp.dot(a, b, preferred_element_type=F32)


def nt(a, b):
    return lax.dot_general(a, b, (((1,), (1,)), ((), ())), preferred_element_type=F32)


def tn(a, b):
    return lax.dot_general(a, b, (((0,), (0,)), ((), ())), preferred_element_type=F32)


def slot_table(ids, y):
    n = ids.shape[1]
    rel = jnp.bitwise_and(ids - y + NY, NY - 1)
    onehot = (lax.broadcasted_iota(jnp.int32, (8, n), 0) == rel).astype(F32)
    earlier = lax.broadcasted_iota(jnp.int32, (n, n), 0) < lax.broadcasted_iota(
        jnp.int32, (n, n), 1
    )
    before = nn(onehot.astype(BF), earlier.astype(F32).astype(BF))
    rank = jnp.sum(before * onehot, axis=0, keepdims=True).astype(jnp.int32)
    slot = rel * CAP + rank
    table = lax.broadcasted_iota(jnp.int32, (NY * CAP, n), 0) == slot
    return table.astype(F32).astype(BF)


def columns(width, step=256):
    return [slice(c, c + step) for c in range(0, width, step)]


def dispatch_kernel(y_ref, *refs):
    ins, outs, scratch, sems = refs[:5], refs[5:9], refs[9:14], refs[14]
    copies = [pltpu.make_async_copy(i, s, sems.at[k]) for k, (i, s) in enumerate(zip(ins, scratch))]
    for c in copies:
        c.start()
    up, down, fwd, saved, grad = scratch
    y = y_ref[0]
    copies[0].wait()
    copies[1].wait()
    table_up = slot_table(up[...], y)
    table_down = slot_table(down[...], y)
    for c in copies[2:]:
        c.wait()
    for c in columns(fwd.shape[1]):
        f = nn(table_up, fwd[:, c])
        s = nn(table_down, saved[:, c])
        g = nn(table_down, grad[:, c])
        pad = jnp.zeros((ROWS - 3 * CAP, f.shape[1]), F32)
        for rel in range(NY):
            r = slice(rel * CAP, (rel + 1) * CAP)
            outs[rel][:, c] = jnp.concatenate([f[r], s[r], g[r], pad], axis=0).astype(BF)


def table_kernel(y_ref, ids_f, ids_b, out_f, out_b):
    n = ids_f.shape[1]
    eye = lax.broadcasted_iota(jnp.int32, (n, n), 0) == lax.broadcasted_iota(
        jnp.int32, (n, n), 1
    )
    eye = eye.astype(F32)
    for ids, out in ((ids_f, out_f), (ids_b, out_b)):
        table = slot_table(ids[...], y_ref[0]).astype(F32)
        for d in range(NY):
            out[d] = nt(eye, table[d * CAP : (d + 1) * CAP]).astype(BF)


def held_kernel(v_ref, *refs):
    out, sem = refs[-2:]
    c = pltpu.make_async_copy(v_ref, out, sem)
    c.start()
    c.wait()


def parts_kernel(left, right, out_a, out_b):
    half = out_a.shape[0]
    out_a[...] = left[:half, :]
    out_b[...] = right[half:, :]


def up_kernel(r0, r1, r2, r3, token, *refs):
    *weights, out = refs
    rows = jnp.concatenate([r[0 : 2 * CAP, :] for r in (r0, r1, r2, r3)], axis=0)
    for i, w in enumerate(weights):
        out[:, i * 256 : (i + 1) * 256] = nn(rows, w[...]).astype(BF)


def up_halves_kernel(r0, r1, r2, r3, wa, wb, out):
    rows = jnp.concatenate([r[0 : 2 * CAP, :] for r in (r0, r1, r2, r3)], axis=0)
    half = wa.shape[0]
    out[...] = (nn(rows[:, :half], wa[...]) + nn(rows[:, half:], wb[...])).astype(BF)


def down_kernel(r0, r1, r2, r3, token, *refs):
    *weights, out = refs
    rows = jnp.concatenate([r[2 * CAP : ROWS, :] for r in (r0, r1, r2, r3)], axis=0)
    at = 0
    for w in weights:
        n = w.shape[0]
        out[:, at : at + n] = nt(rows, w[...]).astype(BF)
        at += n


def pick(v, start, stride):
    return jnp.concatenate(
        [v[i * stride + start : i * stride + start + CAP, :] for i in range(NY)], axis=0
    )


def added(a, b):
    return a.astype(F32) + b.astype(F32)


def activate(pu):
    v = pick(pu, 0, 2 * CAP)
    return (v * jax.nn.sigmoid(v)).astype(BF)


def grad_hidden(pu, pv):
    v = pick(pu, CAP, 2 * CAP)
    g = pick(pv, 0, ROWS - 2 * CAP)
    q = jax.nn.sigmoid(v)
    return (g * (q * (1.0 + v * (1.0 - q)))).astype(BF)


def mid_kernel(r0, r1, r2, r3, pu, qu, pv, qv, u0, u1, u2, v0, v1, v2, acc_f, acc_b):
    su = added(pu[...], qu[...])
    act = activate(su)
    hid = grad_hidden(su, added(pv[...], qv[...]))
    for c in columns(acc_f.shape[1]):
        rows = [r[:, c].astype(F32) for r in (r0, r1, r2, r3)]
        f = jnp.concatenate([r[:CAP] for r in rows], axis=0)
        b = jnp.concatenate([r[2 * CAP : 3 * CAP] for r in rows], axis=0)
        for i, (u, v) in enumerate(((u0, v0), (u1, v1), (u2, v2))):
            f += nn(act[:, i * 256 : (i + 1) * 256], v[:, c])
            b += nt(hid[:, i * 256 : (i + 1) * 256], u[c, :])
        acc_f[:, c] = f
        acc_b[:, c] = b


def last_f_kernel(r0, r1, r2, r3, pu, qu, va, vb, acc, token, out, *outs):
    rows = jnp.concatenate([r[2 * CAP : ROWS, :] for r in (r0, r1, r2, r3)], axis=0)
    half = va.shape[0]
    out[:, :half] = nt(rows, va[...]).astype(BF)
    out[:, half:] = nt(rows, vb[...]).astype(BF)
    act = activate(added(pu[...], qu[...]))
    for c in columns(acc.shape[1]):
        t = acc[:, c] + nn(act[:, :half], va[:, c]) + nn(act[:, half:], vb[:, c])
        for i, o in enumerate(outs):
            o[:, c] = t[i * CAP : (i + 1) * CAP].astype(BF)


def last_b_kernel(pu, qu, pv, qv, ua, ub, acc, token, *outs, parts):
    hid = grad_hidden(added(pu[...], qu[...]), added(pv[...], qv[...]))
    half = ua.shape[0]
    for u, base in ((ua, 0), (ub, half)):
        for c in columns(half, 128):
            o = slice(base + c.start, base + c.stop)
            t = acc[:, o] + nt(hid, u[c, :])
            for i, out in zip(parts, outs):
                out[:, o] = t[i * CAP : (i + 1) * CAP].astype(BF)


def finish_kernel(table, token, total, *refs, parts):
    *rows, out, held, sems = refs
    copies = []
    for i, c in enumerate(columns(out.shape[1])):
        t = total[:, c]
        for d, r in zip(parts, rows):
            t += nn(table[d], r[:, c])
        held[:, c] = t.astype(held.dtype)
        copies.append(pltpu.make_async_copy(held.at[:, c], out.at[:, c], sems.at[i]))
        copies[-1].start()
    for c in copies:
        c.wait()


def combine_kernel(table, token, *refs, parts, first):
    *rows, out = refs if first else refs[1:]
    for c in columns(out.shape[1]):
        t = 0.0 if first else refs[0][:, c]
        for d, r in zip(parts, rows):
            t += nn(table[d], r[:, c])
        out[:, c] = t.astype(out.dtype)


def per_device(
    stream_up, routes_up, cotangent_down, saved_down, routes_down, weight_up, weight_down
):
    u_own = weight_up[0, 0]
    v_own = weight_down[0, 0]
    fwd = stream_up[0]
    cot = cotangent_down[0]
    saved = saved_down[0, 0]
    n, width = fwd.shape
    hp = u_own.shape[1]
    ids_up = routes_up.reshape(1, n)
    ids_down = routes_down.reshape(1, n)
    y = (lax.axis_index("expert") // NX).reshape(1)
    mm = 2 * 320 * width * hp

    def parts(left, right, cost):
        half = sds((left.shape[0] // 2, left.shape[1]))
        return call(
            parts_kernel, [half] * 2, cost, 4 * half.shape[0] * half.shape[1], [VM] * 2, left, right
        )

    u_l, u_r = move_x(u_own, 1), move_x(u_own, -1)
    v_l, v_r = move_x(v_own, 1), move_x(v_own, -1)
    to_r, to_l = parts(u_l, u_r, CU)
    to_u = to_r
    u_a, u_b = move_x(to_r, 1), move_x(to_l, -1)
    to_r, to_l = parts(v_l, v_r, 0)
    to_v = to_r
    v_a, v_b = move_x(to_r, 1), move_x(to_l, -1)

    ids_f, ids_b = move_z(ids_up, 1), move_z(ids_down, -1)
    table_f, table_b = call(
        table_kernel, [sds((NY, n, CAP))] * 2, 0, 4 * NY * CAP * n, [SM, VM, VM], y, ids_f, ids_b
    )

    def held(v, cost, *tokens):
        return call(
            held_kernel,
            sds(v.shape),
            cost,
            4 * ROWS * width,
            [ANY] * (1 + len(tokens)),
            v,
            *tokens,
            scratch=[pltpu.SemaphoreType.DMA],
        )

    sent = call(
        dispatch_kernel,
        [sds((ROWS, width))] * NY,
        6 * 160 * 128 * width,
        7 * 128 * width * 2,
        [SM] + [ANY] * 5,
        y,
        ids_up,
        ids_down,
        fwd,
        saved,
        cot,
        scratch=[pltpu.VMEM((1, n), jnp.int32)] * 2
        + [pltpu.VMEM((n, width), BF)] * 3
        + [pltpu.SemaphoreType.DMA((5,))],
    )
    row2 = move_y(sent[2], 2)
    row1 = move_y(held(sent[1], 0, row2, table_f), 1)
    row3 = move_y(held(sent[3], 0, row1, to_u), 3)
    rows = [sent[0], row1, row2, row3]

    pu = call(
        up_kernel,
        sds((2 * CAP * NY, 3 * hp)),
        3 * mm,
        4 << 20,
        [VM] * 4 + [ANY] + [VM] * 3,
        *rows,
        to_v,
        u_own,
        u_l,
        u_r,
    )
    qu = swap(pu)
    pv = call(
        down_kernel,
        sds(((ROWS - 2 * CAP) * NY, 3 * hp)),
        2 * mm,
        4 << 20,
        [VM] * 4 + [ANY] + [VM] * 3,
        *rows,
        pu,
        v_own,
        v_l,
        v_r,
    )
    qv = swap(pv)
    acc_f, acc_b = call(
        mid_kernel,
        [sds((NY * CAP, width), F32)] * 2,
        3 * mm,
        8 << 20,
        [VM] * 14,
        *rows,
        pu,
        qu,
        pv,
        qv,
        u_own,
        u_l,
        u_r,
        v_own,
        v_l,
        v_r,
    )
    pu2 = call(up_halves_kernel, sds((2 * CAP * NY, hp)), CU2, 2 << 20, [VM] * 6, *rows, u_a, u_b)
    qu2 = swap(pu2)
    pv2, *res_f = call(
        last_f_kernel,
        [sds(((ROWS - 2 * CAP) * NY, hp))] + [sds((CAP, width))] * NY,
        mm,
        2 << 20,
        [VM] * 9 + [ANY],
        *rows,
        pu2,
        qu2,
        v_a,
        v_b,
        acc_f,
        acc_b,
    )
    qv2 = swap(pv2)
    res_b = call(
        functools.partial(last_b_kernel, parts=range(NY)),
        [sds((CAP, width))] * NY,
        mm // 2,
        2 << 20,
        [VM] * 7 + [ANY],
        pu2,
        qu2,
        pv2,
        qv2,
        u_a,
        u_b,
        acc_b,
        res_f[0],
    )
    got_f = [move_zy(r, 1, -d) for d, r in enumerate(res_f)]
    got_b = [move_zy(r, -1, -d) for d, r in enumerate(res_b)]

    def combine(table, got, parts, total, token):
        return call(
            functools.partial(combine_kernel, parts=parts, first=total is None),
            sds((n, width), F32),
            2 * CAP * n * width * len(parts),
            8 * n * width,
            [VM, ANY] + [VM] * (len(parts) + (total is not None)),
            table,
            token,
            *(() if total is None else (total,)),
            *[got[d] for d in parts],
        )

    def finish(table, got, parts, total, token):
        return call(
            functools.partial(finish_kernel, parts=parts),
            sds((n, width)),
            2 * CAP * n * width * len(parts),
            8 * n * width,
            [VM, ANY] + [VM] * (len(parts) + 1),
            table,
            token,
            total,
            *[got[d] for d in parts],
            scratch=[pltpu.VMEM((n, width), BF), pltpu.SemaphoreType.DMA((width // 256,))],
            out_specs=ANY,
        )

    sum_f = combine(table_f, got_f, (0, 2), None, table_b)
    sum_b = combine(table_b, got_b, (0,), None, sum_f)
    sum_f = combine(table_f, got_f, (1,), sum_f, sum_b)
    out_f = finish(table_f, got_f, (3,), sum_f, sum_b)
    sum_b = combine(table_b, got_b, (2, 1), sum_b, sum_f)
    out_b = finish(table_b, got_b, (3,), sum_b, sum_f)
    return (out_f[None], out_b[None])


def solution(mesh):
    return jax.shard_map(
        per_device,
        mesh=mesh,
        in_specs=(
            P("section", "expert", "dp"),
            P("section", None, "expert", None),
            P("section", "expert", "dp"),
            P("section", None, "expert", "dp"),
            P("section", None, "expert", None),
            P("section", "expert", "dp", None),
            P("section", "expert", None, "dp"),
        ),
        out_specs=(P("section", "expert", "dp"), P("section", "expert", "dp")),
        check_vma=False,
    )
```

```python
import functools

import jax
import jax.numpy as jnp
from jax import lax
from jax.experimental import pallas as pl
from jax.experimental.pallas import tpu as pltpu
from jax.sharding import PartitionSpec as P

NX = 4
NY = 4
NZ = 8
CAP = 40
ROWS = 128
BF = jnp.bfloat16
F32 = jnp.float32
VM = pl.BlockSpec(memory_space=pltpu.VMEM)
ANY = pl.BlockSpec(memory_space=pl.ANY)
HBM = pl.BlockSpec(memory_space=pltpu.HBM)
SM = pl.BlockSpec(memory_space=pltpu.SMEM)
CU = 8 * 10**9
CU2 = 6 * 10**9
LIMIT = 24 * 1024 * 1024


def move_x(v, d):
    return lax.ppermute(
        v, "expert", [(y * NX + x, y * NX + (x + d) % NX) for y in range(NY) for x in range(NX)]
    )


def move_y(v, d):
    return lax.ppermute(
        v, "expert", [(y * NX + x, (y + d) % NY * NX + x) for y in range(NY) for x in range(NX)]
    )


def move_z(v, d):
    return lax.ppermute(v, "section", [(z, (z + d) % NZ) for z in range(NZ)])


def move_zy(v, dz, dy):
    n = NX * NY
    pairs = [
        (z * n + y * NX + x, (z + dz) % NZ * n + (y + dy) % NY * NX + x)
        for z in range(NZ)
        for y in range(NY)
        for x in range(NX)
    ]
    return lax.ppermute(v, ("section", "expert"), pairs)


def swap(v):
    return lax.ppermute(v, "dp", [(0, 1), (1, 0)])


def call(kernel, outs, flops, nbytes, in_specs, *args, scratch=(), out_specs=None):
    return pl.pallas_call(
        kernel,
        out_shape=outs,
        scratch_shapes=scratch,
        in_specs=in_specs,
        out_specs=out_specs or jax.tree.map(lambda _: VM, outs),
        compiler_params=pltpu.CompilerParams(vmem_limit_bytes=LIMIT),
        cost_estimate=pl.CostEstimate(flops=flops, bytes_accessed=nbytes, transcendentals=0),
    )(*args)


def sds(shape, dtype=BF):
    return jax.ShapeDtypeStruct(shape, dtype)


def nn(a, b):
    return jnp.dot(a, b, preferred_element_type=F32)


def nt(a, b):
    return lax.dot_general(a, b, (((1,), (1,)), ((), ())), preferred_element_type=F32)


def tn(a, b):
    return lax.dot_general(a, b, (((0,), (0,)), ((), ())), preferred_element_type=F32)


def slot_table(ids, y):
    n = ids.shape[1]
    rel = jnp.bitwise_and(ids - y + NY, NY - 1)
    onehot = (lax.broadcasted_iota(jnp.int32, (8, n), 0) == rel).astype(F32)
    earlier = lax.broadcasted_iota(jnp.int32, (n, n), 0) < lax.broadcasted_iota(
        jnp.int32, (n, n), 1
    )
    before = nn(onehot.astype(BF), earlier.astype(F32).astype(BF))
    rank = jnp.sum(before * onehot, axis=0, keepdims=True).astype(jnp.int32)
    slot = rel * CAP + rank
    table = lax.broadcasted_iota(jnp.int32, (NY * CAP, n), 0) == slot
    return table.astype(F32).astype(BF)


def columns(width, step=256):
    return [slice(c, c + step) for c in range(0, width, step)]


def dispatch_kernel(y_ref, *refs):
    ins, outs, scratch, sems = refs[:5], refs[5:9], refs[9:14], refs[14]
    copies = [pltpu.make_async_copy(i, s, sems.at[k]) for k, (i, s) in enumerate(zip(ins, scratch))]
    for c in copies:
        c.start()
    up, down, fwd, saved, grad = scratch
    y = y_ref[0]
    copies[0].wait()
    copies[1].wait()
    table_up = slot_table(up[...], y)
    table_down = slot_table(down[...], y)
    for c in copies[2:]:
        c.wait()
    for c in columns(fwd.shape[1]):
        f = nn(table_up, fwd[:, c])
        s = nn(table_down, saved[:, c])
        g = nn(table_down, grad[:, c])
        pad = jnp.zeros((ROWS - 3 * CAP, f.shape[1]), F32)
        for rel in range(NY):
            r = slice(rel * CAP, (rel + 1) * CAP)
            outs[rel][:, c] = jnp.concatenate([f[r], s[r], g[r], pad], axis=0).astype(BF)


def table_kernel(y_ref, ids_f, ids_b, out_f, out_b):
    n = ids_f.shape[1]
    eye = lax.broadcasted_iota(jnp.int32, (n, n), 0) == lax.broadcasted_iota(
        jnp.int32, (n, n), 1
    )
    eye = eye.astype(F32)
    for ids, out in ((ids_f, out_f), (ids_b, out_b)):
        table = slot_table(ids[...], y_ref[0]).astype(F32)
        for d in range(NY):
            out[d] = nt(eye, table[d * CAP : (d + 1) * CAP]).astype(BF)


def held_kernel(v_ref, *refs):
    out, sem = refs[-2:]
    c = pltpu.make_async_copy(v_ref, out, sem)
    c.start()
    c.wait()


def parts_kernel(left, right, out_a, out_b):
    half = out_a.shape[0]
    out_a[...] = left[:half, :]
    out_b[...] = right[half:, :]


def up_kernel(r0, r1, r2, r3, token, *refs):
    *weights, out = refs
    rows = jnp.concatenate([r[0 : 2 * CAP, :] for r in (r0, r1, r2, r3)], axis=0)
    for i, w in enumerate(weights):
        out[:, i * 256 : (i + 1) * 256] = nn(rows, w[...]).astype(BF)


def up_halves_kernel(r0, r1, r2, r3, wa, wb, out):
    rows = jnp.concatenate([r[0 : 2 * CAP, :] for r in (r0, r1, r2, r3)], axis=0)
    half = wa.shape[0]
    out[...] = (nn(rows[:, :half], wa[...]) + nn(rows[:, half:], wb[...])).astype(BF)


def down_kernel(r0, r1, r2, r3, token, *refs):
    *weights, out = refs
    rows = jnp.concatenate([r[2 * CAP : ROWS, :] for r in (r0, r1, r2, r3)], axis=0)
    at = 0
    for w in weights:
        n = w.shape[0]
        out[:, at : at + n] = nt(rows, w[...]).astype(BF)
        at += n


def pick(v, start, stride):
    return jnp.concatenate(
        [v[i * stride + start : i * stride + start + CAP, :] for i in range(NY)], axis=0
    )


def added(a, b):
    return a.astype(F32) + b.astype(F32)


def activate(pu):
    v = pick(pu, 0, 2 * CAP)
    return (v * jax.nn.sigmoid(v)).astype(BF)


def grad_hidden(pu, pv):
    v = pick(pu, CAP, 2 * CAP)
    g = pick(pv, 0, ROWS - 2 * CAP)
    q = jax.nn.sigmoid(v)
    return (g * (q * (1.0 + v * (1.0 - q)))).astype(BF)


def mid_kernel(r0, r1, r2, r3, pu, qu, pv, qv, u0, u1, u2, v0, v1, v2, acc_f, acc_b):
    su = added(pu[...], qu[...])
    act = activate(su)
    hid = grad_hidden(su, added(pv[...], qv[...]))
    for c in columns(acc_f.shape[1]):
        rows = [r[:, c].astype(F32) for r in (r0, r1, r2, r3)]
        f = jnp.concatenate([r[:CAP] for r in rows], axis=0)
        b = jnp.concatenate([r[2 * CAP : 3 * CAP] for r in rows], axis=0)
        for i, (u, v) in enumerate(((u0, v0), (u1, v1), (u2, v2))):
            f += nn(act[:, i * 256 : (i + 1) * 256], v[:, c])
            b += nt(hid[:, i * 256 : (i + 1) * 256], u[c, :])
        acc_f[:, c] = f
        acc_b[:, c] = b


def last_f_kernel(r0, r1, r2, r3, pu, qu, va, vb, acc, token, out, *outs):
    rows = jnp.concatenate([r[2 * CAP : ROWS, :] for r in (r0, r1, r2, r3)], axis=0)
    half = va.shape[0]
    out[:, :half] = nt(rows, va[...]).astype(BF)
    out[:, half:] = nt(rows, vb[...]).astype(BF)
    act = activate(added(pu[...], qu[...]))
    for c in columns(acc.shape[1]):
        t = acc[:, c] + nn(act[:, :half], va[:, c]) + nn(act[:, half:], vb[:, c])
        for i, o in enumerate(outs):
            o[:, c] = t[i * CAP : (i + 1) * CAP].astype(BF)


def last_b_kernel(pu, qu, pv, qv, ua, ub, acc, token, *outs, parts):
    hid = grad_hidden(added(pu[...], qu[...]), added(pv[...], qv[...]))
    half = ua.shape[0]
    for u, base in ((ua, 0), (ub, half)):
        for c in columns(half, 128):
            o = slice(base + c.start, base + c.stop)
            t = acc[:, o] + nt(hid, u[c, :])
            for i, out in zip(parts, outs):
                out[:, o] = t[i * CAP : (i + 1) * CAP].astype(BF)


def finish_kernel(table, total_f, total_b, row, *refs, stream, group):
    outs, held, sems = refs[:2], refs[2], refs[3]
    copies = []
    for k in (1 - stream, stream):
        total = (total_f, total_b)[k]
        for i, c in enumerate(columns(total.shape[1])):
            t = total[:, c]
            if k == stream:
                t += nn(table[group], row[:, c])
            held[k, :, c] = t.astype(held.dtype)
            copies.append(
                pltpu.make_async_copy(held.at[k, :, c], outs[k].at[:, c], sems.at[k, i])
            )
            copies[-1].start()
    for c in copies:
        c.wait()


def combine_kernel(table, token, *refs, parts, first):
    *rows, out = refs if first else refs[1:]
    for c in columns(out.shape[1]):
        t = 0.0 if first else refs[0][:, c]
        for d, r in zip(parts, rows):
            t += nn(table[d], r[:, c])
        out[:, c] = t.astype(out.dtype)


def per_device(
    stream_up, routes_up, cotangent_down, saved_down, routes_down, weight_up, weight_down
):
    u_own = weight_up[0, 0]
    v_own = weight_down[0, 0]
    fwd = stream_up[0]
    cot = cotangent_down[0]
    saved = saved_down[0, 0]
    n, width = fwd.shape
    hp = u_own.shape[1]
    ids_up = routes_up.reshape(1, n)
    ids_down = routes_down.reshape(1, n)
    y = (lax.axis_index("expert") // NX).reshape(1)
    mm = 2 * 320 * width * hp

    def parts(left, right, cost):
        half = sds((left.shape[0] // 2, left.shape[1]))
        return call(
            parts_kernel, [half] * 2, cost, 4 * half.shape[0] * half.shape[1], [VM] * 2, left, right
        )

    u_l, u_r = move_x(u_own, 1), move_x(u_own, -1)
    v_l, v_r = move_x(v_own, 1), move_x(v_own, -1)
    to_r, to_l = parts(u_l, u_r, CU)
    to_u = to_r
    u_a, u_b = move_x(to_r, 1), move_x(to_l, -1)
    to_r, to_l = parts(v_l, v_r, 0)
    to_v = to_r
    v_a, v_b = move_x(to_r, 1), move_x(to_l, -1)

    ids_f, ids_b = move_z(ids_up, 1), move_z(ids_down, -1)
    table_f, table_b = call(
        table_kernel, [sds((NY, n, CAP))] * 2, 0, 4 * NY * CAP * n, [SM, VM, VM], y, ids_f, ids_b
    )

    def held(v, cost, *tokens):
        return call(
            held_kernel,
            sds(v.shape),
            cost,
            4 * ROWS * width,
            [ANY] * (1 + len(tokens)),
            v,
            *tokens,
            scratch=[pltpu.SemaphoreType.DMA],
        )

    sent = call(
        dispatch_kernel,
        [sds((ROWS, width))] * NY,
        6 * 160 * 128 * width,
        7 * 128 * width * 2,
        [SM] + [ANY] * 5,
        y,
        ids_up,
        ids_down,
        fwd,
        saved,
        cot,
        scratch=[pltpu.VMEM((1, n), jnp.int32)] * 2
        + [pltpu.VMEM((n, width), BF)] * 3
        + [pltpu.SemaphoreType.DMA((5,))],
    )
    row2 = move_y(sent[2], 2)
    row1 = move_y(held(sent[1], 0, row2, table_f), 1)
    row3 = move_y(held(sent[3], 0, row1, to_u), 3)
    rows = [sent[0], row1, row2, row3]

    pu = call(
        up_kernel,
        sds((2 * CAP * NY, 3 * hp)),
        3 * mm,
        4 << 20,
        [VM] * 4 + [ANY] + [VM] * 3,
        *rows,
        to_v,
        u_own,
        u_l,
        u_r,
    )
    qu = swap(pu)
    pv = call(
        down_kernel,
        sds(((ROWS - 2 * CAP) * NY, 3 * hp)),
        2 * mm,
        4 << 20,
        [VM] * 4 + [ANY] + [VM] * 3,
        *rows,
        pu,
        v_own,
        v_l,
        v_r,
    )
    qv = swap(pv)
    acc_f, acc_b = call(
        mid_kernel,
        [sds((NY * CAP, width), F32)] * 2,
        3 * mm,
        8 << 20,
        [VM] * 14,
        *rows,
        pu,
        qu,
        pv,
        qv,
        u_own,
        u_l,
        u_r,
        v_own,
        v_l,
        v_r,
    )
    pu2 = call(up_halves_kernel, sds((2 * CAP * NY, hp)), CU2, 2 << 20, [VM] * 6, *rows, u_a, u_b)
    qu2 = swap(pu2)
    pv2, *res_f = call(
        last_f_kernel,
        [sds(((ROWS - 2 * CAP) * NY, hp))] + [sds((CAP, width))] * NY,
        mm,
        2 << 20,
        [VM] * 9 + [ANY],
        *rows,
        pu2,
        qu2,
        v_a,
        v_b,
        acc_f,
        acc_b,
    )
    qv2 = swap(pv2)
    res_b = call(
        functools.partial(last_b_kernel, parts=range(NY)),
        [sds((CAP, width))] * NY,
        mm // 2,
        2 << 20,
        [VM] * 7 + [ANY],
        pu2,
        qu2,
        pv2,
        qv2,
        u_a,
        u_b,
        acc_b,
        res_f[0],
    )
    got_f = [move_zy(r, 1, -d) for d, r in enumerate(res_f)]
    got_b = [move_zy(r, -1, -d) for d, r in enumerate(res_b)]

    def combine(table, got, parts, total, token):
        return call(
            functools.partial(combine_kernel, parts=parts, first=total is None),
            sds((n, width), F32),
            2 * CAP * n * width * len(parts),
            8 * n * width,
            [VM, ANY] + [VM] * (len(parts) + (total is not None)),
            table,
            token,
            *(() if total is None else (total,)),
            *[got[d] for d in parts],
        )

    def finish(total_f, total_b, stream, group):
        return call(
            functools.partial(finish_kernel, stream=stream, group=group),
            [sds((n, width))] * 2,
            2 * CAP * n * width,
            12 * n * width,
            [VM] * 4,
            (table_f, table_b)[stream],
            total_f,
            total_b,
            (got_f, got_b)[stream][group],
            scratch=[
                pltpu.VMEM((2, n, width), BF),
                pltpu.SemaphoreType.DMA((2, width // 256)),
            ],
            out_specs=[ANY, ANY],
        )

    sum_f = combine(table_f, got_f, (2,), None, table_b)
    sum_b = combine(table_b, got_b, (3,), None, sum_f)
    sum_f = combine(table_f, got_f, (1,), sum_f, sum_b)
    sum_b = combine(table_b, got_b, (0,), sum_b, sum_f)
    sum_f = combine(table_f, got_f, (3,), sum_f, sum_b)
    sum_b = combine(table_b, got_b, (1,), sum_b, sum_f)
    sum_b = combine(table_b, got_b, (2,), sum_b, sum_b)
    out_f, out_b = finish(sum_f, sum_b, 0, 0)
    return (out_f[None], out_b[None])


def solution(mesh):
    return jax.shard_map(
        per_device,
        mesh=mesh,
        in_specs=(
            P("section", "expert", "dp"),
            P("section", None, "expert", None),
            P("section", "expert", "dp"),
            P("section", None, "expert", "dp"),
            P("section", None, "expert", None),
            P("section", "expert", "dp", None),
            P("section", "expert", None, "dp"),
        ),
        out_specs=(P("section", "expert", "dp"), P("section", "expert", "dp")),
        check_vma=False,
    )
```

```python
import functools

import jax
import jax.numpy as jnp
from jax import lax
from jax.experimental import pallas as pl
from jax.experimental.pallas import tpu as pltpu
from jax.sharding import PartitionSpec as P

NX = 4
NY = 4
NZ = 8
CAP = 40
ROWS = 128
BF = jnp.bfloat16
F32 = jnp.float32
VM = pl.BlockSpec(memory_space=pltpu.VMEM)
ANY = pl.BlockSpec(memory_space=pl.ANY)
HBM = pl.BlockSpec(memory_space=pltpu.HBM)
SM = pl.BlockSpec(memory_space=pltpu.SMEM)
CU = 8 * 10**9
CU2 = 6 * 10**9
LIMIT = 24 * 1024 * 1024


def move_x(v, d):
    return lax.ppermute(
        v, "expert", [(y * NX + x, y * NX + (x + d) % NX) for y in range(NY) for x in range(NX)]
    )


def move_y(v, d):
    return lax.ppermute(
        v, "expert", [(y * NX + x, (y + d) % NY * NX + x) for y in range(NY) for x in range(NX)]
    )


def move_z(v, d):
    return lax.ppermute(v, "section", [(z, (z + d) % NZ) for z in range(NZ)])


def move_zy(v, dz, dy):
    n = NX * NY
    pairs = [
        (z * n + y * NX + x, (z + dz) % NZ * n + (y + dy) % NY * NX + x)
        for z in range(NZ)
        for y in range(NY)
        for x in range(NX)
    ]
    return lax.ppermute(v, ("section", "expert"), pairs)


def swap(v):
    return lax.ppermute(v, "dp", [(0, 1), (1, 0)])


def call(kernel, outs, flops, nbytes, in_specs, *args, scratch=(), out_specs=None):
    return pl.pallas_call(
        kernel,
        out_shape=outs,
        scratch_shapes=scratch,
        in_specs=in_specs,
        out_specs=out_specs or jax.tree.map(lambda _: VM, outs),
        compiler_params=pltpu.CompilerParams(vmem_limit_bytes=LIMIT),
        cost_estimate=pl.CostEstimate(flops=flops, bytes_accessed=nbytes, transcendentals=0),
    )(*args)


def sds(shape, dtype=BF):
    return jax.ShapeDtypeStruct(shape, dtype)


def nn(a, b):
    return jnp.dot(a, b, preferred_element_type=F32)


def nt(a, b):
    return lax.dot_general(a, b, (((1,), (1,)), ((), ())), preferred_element_type=F32)


def tn(a, b):
    return lax.dot_general(a, b, (((0,), (0,)), ((), ())), preferred_element_type=F32)


def slot_table(ids, y):
    n = ids.shape[1]
    rel = jnp.bitwise_and(ids - y + NY, NY - 1)
    onehot = (lax.broadcasted_iota(jnp.int32, (8, n), 0) == rel).astype(F32)
    earlier = lax.broadcasted_iota(jnp.int32, (n, n), 0) < lax.broadcasted_iota(
        jnp.int32, (n, n), 1
    )
    before = nn(onehot.astype(BF), earlier.astype(F32).astype(BF))
    rank = jnp.sum(before * onehot, axis=0, keepdims=True).astype(jnp.int32)
    slot = rel * CAP + rank
    table = lax.broadcasted_iota(jnp.int32, (NY * CAP, n), 0) == slot
    return table.astype(F32).astype(BF)


def columns(width, step=256):
    return [slice(c, c + step) for c in range(0, width, step)]


def dispatch_kernel(y_ref, *refs):
    ins, outs, scratch, sems = refs[:5], refs[5:9], refs[9:14], refs[14]
    copies = [pltpu.make_async_copy(i, s, sems.at[k]) for k, (i, s) in enumerate(zip(ins, scratch))]
    for c in copies:
        c.start()
    up, down, fwd, saved, grad = scratch
    y = y_ref[0]
    copies[0].wait()
    copies[1].wait()
    table_up = slot_table(up[...], y)
    table_down = slot_table(down[...], y)
    for c in copies[2:]:
        c.wait()
    for c in columns(fwd.shape[1]):
        f = nn(table_up, fwd[:, c])
        s = nn(table_down, saved[:, c])
        g = nn(table_down, grad[:, c])
        pad = jnp.zeros((ROWS - 3 * CAP, f.shape[1]), F32)
        for rel in range(NY):
            r = slice(rel * CAP, (rel + 1) * CAP)
            outs[rel][:, c] = jnp.concatenate([f[r], s[r], g[r], pad], axis=0).astype(BF)


def table_kernel(y_ref, ids_f, ids_b, out_f, out_b):
    n = ids_f.shape[1]
    eye = lax.broadcasted_iota(jnp.int32, (n, n), 0) == lax.broadcasted_iota(
        jnp.int32, (n, n), 1
    )
    eye = eye.astype(F32)
    for ids, out in ((ids_f, out_f), (ids_b, out_b)):
        table = slot_table(ids[...], y_ref[0]).astype(F32)
        for d in range(NY):
            out[d] = nt(eye, table[d * CAP : (d + 1) * CAP]).astype(BF)


def held_kernel(v_ref, *refs):
    out, sem = refs[-2:]
    c = pltpu.make_async_copy(v_ref, out, sem)
    c.start()
    c.wait()


def parts_kernel(left, right, out_a, out_b):
    half = out_a.shape[0]
    out_a[...] = left[:half, :]
    out_b[...] = right[half:, :]


def up_kernel(r0, r1, r2, r3, token, *refs):
    *weights, out = refs
    rows = jnp.concatenate([r[0 : 2 * CAP, :] for r in (r0, r1, r2, r3)], axis=0)
    for i, w in enumerate(weights):
        out[:, i * 256 : (i + 1) * 256] = nn(rows, w[...]).astype(BF)


def up_halves_kernel(r0, r1, r2, r3, wa, wb, out):
    rows = jnp.concatenate([r[0 : 2 * CAP, :] for r in (r0, r1, r2, r3)], axis=0)
    half = wa.shape[0]
    out[...] = (nn(rows[:, :half], wa[...]) + nn(rows[:, half:], wb[...])).astype(BF)


def down_kernel(r0, r1, r2, r3, token, *refs):
    *weights, out = refs
    rows = jnp.concatenate([r[2 * CAP : ROWS, :] for r in (r0, r1, r2, r3)], axis=0)
    at = 0
    for w in weights:
        n = w.shape[0]
        out[:, at : at + n] = nt(rows, w[...]).astype(BF)
        at += n


def pick(v, start, stride):
    return jnp.concatenate(
        [v[i * stride + start : i * stride + start + CAP, :] for i in range(NY)], axis=0
    )


def added(a, b):
    return a.astype(F32) + b.astype(F32)


def activate(pu):
    v = pick(pu, 0, 2 * CAP)
    return (v * jax.nn.sigmoid(v)).astype(BF)


def grad_hidden(pu, pv):
    v = pick(pu, CAP, 2 * CAP)
    g = pick(pv, 0, ROWS - 2 * CAP)
    q = jax.nn.sigmoid(v)
    return (g * (q * (1.0 + v * (1.0 - q)))).astype(BF)


def mid_kernel(r0, r1, r2, r3, pu, qu, pv, qv, u0, u1, u2, v0, v1, v2, acc_f, acc_b):
    su = added(pu[...], qu[...])
    act = activate(su)
    hid = grad_hidden(su, added(pv[...], qv[...]))
    for c in columns(acc_f.shape[1]):
        rows = [r[:, c].astype(F32) for r in (r0, r1, r2, r3)]
        f = jnp.concatenate([r[:CAP] for r in rows], axis=0)
        b = jnp.concatenate([r[2 * CAP : 3 * CAP] for r in rows], axis=0)
        for i, (u, v) in enumerate(((u0, v0), (u1, v1), (u2, v2))):
            f += nn(act[:, i * 256 : (i + 1) * 256], v[:, c])
            b += nt(hid[:, i * 256 : (i + 1) * 256], u[c, :])
        acc_f[:, c] = f
        acc_b[:, c] = b


def last_f_kernel(r0, r1, r2, r3, pu, qu, va, vb, acc, token, out, *outs):
    rows = jnp.concatenate([r[2 * CAP : ROWS, :] for r in (r0, r1, r2, r3)], axis=0)
    out[...] = nt(rows, jnp.concatenate([va[...], vb[...]], axis=0)).astype(BF)
    act = activate(added(pu[...], qu[...]))
    for c in columns(acc.shape[1]):
        t = acc[:, c] + nn(act, jnp.concatenate([va[:, c], vb[:, c]], axis=0))
        for i, o in enumerate(outs):
            o[:, c] = t[i * CAP : (i + 1) * CAP].astype(BF)


def last_b_kernel(pu, qu, pv, qv, ua, ub, acc, token, *outs, parts):
    hid = grad_hidden(added(pu[...], qu[...]), added(pv[...], qv[...]))
    half = ua.shape[0]
    for c in columns(acc.shape[1]):
        pieces = []
        if c.start < half:
            pieces.append(ua[c.start : min(c.stop, half), :])
        if c.stop > half:
            pieces.append(ub[max(c.start, half) - half : c.stop - half, :])
        t = acc[:, c] + nt(hid, jnp.concatenate(pieces, axis=0))
        for i, out in zip(parts, outs):
            out[:, c] = t[i * CAP : (i + 1) * CAP].astype(BF)


def finish_kernel(table, total_f, total_b, row, *refs, stream, group):
    outs, held, sems = refs[:2], refs[2], refs[3]
    copies = []
    for k in (1 - stream, stream):
        total = (total_f, total_b)[k]
        for c in columns(total.shape[1]):
            t = total[:, c]
            if k == stream:
                t += nn(table[group], row[:, c])
            held[k, :, c] = t.astype(held.dtype)
        copies.append(pltpu.make_async_copy(held.at[k], outs[k], sems.at[k]))
        copies[-1].start()
    for c in copies:
        c.wait()


def combine_kernel(table, token, *refs, parts, first):
    *rows, out = refs if first else refs[1:]
    for c in columns(out.shape[1]):
        t = 0.0 if first else refs[0][:, c]
        for d, r in zip(parts, rows):
            t += nn(table[d], r[:, c])
        out[:, c] = t.astype(out.dtype)


def per_device(
    stream_up, routes_up, cotangent_down, saved_down, routes_down, weight_up, weight_down
):
    u_own = weight_up[0, 0]
    v_own = weight_down[0, 0]
    fwd = stream_up[0]
    cot = cotangent_down[0]
    saved = saved_down[0, 0]
    n, width = fwd.shape
    hp = u_own.shape[1]
    ids_up = routes_up.reshape(1, n)
    ids_down = routes_down.reshape(1, n)
    y = (lax.axis_index("expert") // NX).reshape(1)
    mm = 2 * 320 * width * hp

    def parts(left, right, cost):
        half = sds((left.shape[0] // 2, left.shape[1]))
        return call(
            parts_kernel, [half] * 2, cost, 4 * half.shape[0] * half.shape[1], [VM] * 2, left, right
        )

    u_l, u_r = move_x(u_own, 1), move_x(u_own, -1)
    v_l, v_r = move_x(v_own, 1), move_x(v_own, -1)
    to_r, to_l = parts(u_l, u_r, CU)
    to_u = to_r
    u_a, u_b = move_x(to_r, 1), move_x(to_l, -1)
    to_r, to_l = parts(v_l, v_r, 0)
    to_v = to_r
    v_a, v_b = move_x(to_r, 1), move_x(to_l, -1)

    ids_f, ids_b = move_z(ids_up, 1), move_z(ids_down, -1)
    table_f, table_b = call(
        table_kernel, [sds((NY, n, CAP))] * 2, 0, 4 * NY * CAP * n, [SM, VM, VM], y, ids_f, ids_b
    )

    def held(v, cost, *tokens):
        return call(
            held_kernel,
            sds(v.shape),
            cost,
            4 * ROWS * width,
            [ANY] * (1 + len(tokens)),
            v,
            *tokens,
            scratch=[pltpu.SemaphoreType.DMA],
        )

    sent = call(
        dispatch_kernel,
        [sds((ROWS, width))] * NY,
        6 * 160 * 128 * width,
        7 * 128 * width * 2,
        [SM] + [ANY] * 5,
        y,
        ids_up,
        ids_down,
        fwd,
        saved,
        cot,
        scratch=[pltpu.VMEM((1, n), jnp.int32)] * 2
        + [pltpu.VMEM((n, width), BF)] * 3
        + [pltpu.SemaphoreType.DMA((5,))],
    )
    row2 = move_y(sent[2], 2)
    row1 = move_y(held(sent[1], 0, row2, table_f), 1)
    row3 = move_y(held(sent[3], 0, row1, to_u), 3)
    rows = [sent[0], row1, row2, row3]

    pu = call(
        up_kernel,
        sds((2 * CAP * NY, 3 * hp)),
        3 * mm,
        4 << 20,
        [VM] * 4 + [ANY] + [VM] * 3,
        *rows,
        to_v,
        u_own,
        u_l,
        u_r,
    )
    qu = swap(pu)
    pv = call(
        down_kernel,
        sds(((ROWS - 2 * CAP) * NY, 3 * hp)),
        2 * mm,
        4 << 20,
        [VM] * 4 + [ANY] + [VM] * 3,
        *rows,
        pu,
        v_own,
        v_l,
        v_r,
    )
    qv = swap(pv)
    acc_f, acc_b = call(
        mid_kernel,
        [sds((NY * CAP, width), F32)] * 2,
        3 * mm,
        8 << 20,
        [VM] * 14,
        *rows,
        pu,
        qu,
        pv,
        qv,
        u_own,
        u_l,
        u_r,
        v_own,
        v_l,
        v_r,
    )
    pu2 = call(up_halves_kernel, sds((2 * CAP * NY, hp)), CU2, 2 << 20, [VM] * 6, *rows, u_a, u_b)
    qu2 = swap(pu2)
    pv2, *res_f = call(
        last_f_kernel,
        [sds(((ROWS - 2 * CAP) * NY, hp))] + [sds((CAP, width))] * NY,
        mm,
        2 << 20,
        [VM] * 9 + [ANY],
        *rows,
        pu2,
        qu2,
        v_a,
        v_b,
        acc_f,
        acc_b,
    )
    qv2 = swap(pv2)
    res_b = call(
        functools.partial(last_b_kernel, parts=range(NY)),
        [sds((CAP, width))] * NY,
        mm // 2,
        2 << 20,
        [VM] * 7 + [ANY],
        pu2,
        qu2,
        pv2,
        qv2,
        u_a,
        u_b,
        acc_b,
        res_f[0],
    )
    got_f = [move_zy(r, 1, -d) for d, r in enumerate(res_f)]
    got_b = [move_zy(r, -1, -d) for d, r in enumerate(res_b)]

    def combine(table, got, parts, total, token):
        return call(
            functools.partial(combine_kernel, parts=parts, first=total is None),
            sds((n, width), F32),
            2 * CAP * n * width * len(parts),
            8 * n * width,
            [VM, ANY] + [VM] * (len(parts) + (total is not None)),
            table,
            token,
            *(() if total is None else (total,)),
            *[got[d] for d in parts],
        )

    def finish(total_f, total_b, stream, group):
        return call(
            functools.partial(finish_kernel, stream=stream, group=group),
            [sds((n, width))] * 2,
            2 * CAP * n * width,
            12 * n * width,
            [VM] * 4,
            (table_f, table_b)[stream],
            total_f,
            total_b,
            (got_f, got_b)[stream][group],
            scratch=[
                pltpu.VMEM((2, n, width), BF),
                pltpu.SemaphoreType.DMA((2,)),
            ],
            out_specs=[ANY, ANY],
        )

    sum_f = combine(table_f, got_f, (2,), None, table_b)
    sum_b = combine(table_b, got_b, (3,), None, sum_f)
    sum_f = combine(table_f, got_f, (1,), sum_f, sum_b)
    sum_b = combine(table_b, got_b, (0,), sum_b, sum_f)
    sum_f = combine(table_f, got_f, (3,), sum_f, sum_b)
    sum_b = combine(table_b, got_b, (1,), sum_b, sum_f)
    sum_b = combine(table_b, got_b, (2,), sum_b, sum_b)
    out_f, out_b = finish(sum_f, sum_b, 0, 0)
    return (out_f[None], out_b[None])


def solution(mesh):
    return jax.shard_map(
        per_device,
        mesh=mesh,
        in_specs=(
            P("section", "expert", "dp"),
            P("section", None, "expert", None),
            P("section", "expert", "dp"),
            P("section", None, "expert", "dp"),
            P("section", None, "expert", None),
            P("section", "expert", "dp", None),
            P("section", "expert", None, "dp"),
        ),
        out_specs=(P("section", "expert", "dp"), P("section", "expert", "dp")),
        check_vma=False,
    )
```

```python
import functools

import jax
import jax.numpy as jnp
from jax import lax
from jax.experimental import pallas as pl
from jax.experimental.pallas import tpu as pltpu
from jax.sharding import PartitionSpec as P

NX = 4
NY = 4
NZ = 8
CAP = 40
ROWS = 128
BF = jnp.bfloat16
F32 = jnp.float32
VM = pl.BlockSpec(memory_space=pltpu.VMEM)
ANY = pl.BlockSpec(memory_space=pl.ANY)
HBM = pl.BlockSpec(memory_space=pltpu.HBM)
SM = pl.BlockSpec(memory_space=pltpu.SMEM)
CU = 8 * 10**9
CU2 = 6 * 10**9
LIMIT = 24 * 1024 * 1024


def move_x(v, d):
    return lax.ppermute(
        v, "expert", [(y * NX + x, y * NX + (x + d) % NX) for y in range(NY) for x in range(NX)]
    )


def move_x_cores(v, d):
    pairs = [
        ((y * NX + x) * 2 + c, (y * NX + (x + d * (1 - 2 * c)) % NX) * 2 + c)
        for y in range(NY)
        for x in range(NX)
        for c in range(2)
    ]
    return lax.ppermute(v, ("expert", "dp"), pairs)


def move_y(v, d):
    return lax.ppermute(
        v, "expert", [(y * NX + x, (y + d) % NY * NX + x) for y in range(NY) for x in range(NX)]
    )


def move_z(v, d):
    return lax.ppermute(v, "section", [(z, (z + d) % NZ) for z in range(NZ)])


def move_zy(v, dz, dy):
    n = NX * NY
    pairs = [
        (z * n + y * NX + x, (z + dz) % NZ * n + (y + dy) % NY * NX + x)
        for z in range(NZ)
        for y in range(NY)
        for x in range(NX)
    ]
    return lax.ppermute(v, ("section", "expert"), pairs)


def swap(v):
    return lax.ppermute(v, "dp", [(0, 1), (1, 0)])


def call(kernel, outs, flops, nbytes, in_specs, *args, scratch=(), out_specs=None):
    return pl.pallas_call(
        kernel,
        out_shape=outs,
        scratch_shapes=scratch,
        in_specs=in_specs,
        out_specs=out_specs or jax.tree.map(lambda _: VM, outs),
        compiler_params=pltpu.CompilerParams(vmem_limit_bytes=LIMIT),
        cost_estimate=pl.CostEstimate(flops=flops, bytes_accessed=nbytes, transcendentals=0),
    )(*args)


def sds(shape, dtype=BF):
    return jax.ShapeDtypeStruct(shape, dtype)


def nn(a, b):
    return jnp.dot(a, b, preferred_element_type=F32)


def nt(a, b):
    return lax.dot_general(a, b, (((1,), (1,)), ((), ())), preferred_element_type=F32)


def tn(a, b):
    return lax.dot_general(a, b, (((0,), (0,)), ((), ())), preferred_element_type=F32)


def slot_table(ids, y):
    n = ids.shape[1]
    rel = jnp.bitwise_and(ids - y + NY, NY - 1)
    onehot = (lax.broadcasted_iota(jnp.int32, (8, n), 0) == rel).astype(F32)
    earlier = lax.broadcasted_iota(jnp.int32, (n, n), 0) < lax.broadcasted_iota(
        jnp.int32, (n, n), 1
    )
    before = nn(onehot.astype(BF), earlier.astype(F32).astype(BF))
    rank = jnp.sum(before * onehot, axis=0, keepdims=True).astype(jnp.int32)
    slot = rel * CAP + rank
    table = lax.broadcasted_iota(jnp.int32, (NY * CAP, n), 0) == slot
    return table.astype(F32).astype(BF)


def columns(width, step=256):
    return [slice(c, c + step) for c in range(0, width, step)]


def dispatch_kernel(y_ref, *refs):
    ins, outs, scratch, sems = refs[:5], refs[5:9], refs[9:14], refs[14]
    copies = [pltpu.make_async_copy(i, s, sems.at[k]) for k, (i, s) in enumerate(zip(ins, scratch))]
    for c in copies:
        c.start()
    up, down, fwd, saved, grad = scratch
    y = y_ref[0]
    copies[0].wait()
    copies[1].wait()
    table_up = slot_table(up[...], y)
    table_down = slot_table(down[...], y)
    for c in copies[2:]:
        c.wait()
    for c in columns(fwd.shape[1]):
        f = nn(table_up, fwd[:, c])
        s = nn(table_down, saved[:, c])
        g = nn(table_down, grad[:, c])
        pad = jnp.zeros((ROWS - 3 * CAP, f.shape[1]), F32)
        for rel in range(NY):
            r = slice(rel * CAP, (rel + 1) * CAP)
            outs[rel][:, c] = jnp.concatenate([f[r], s[r], g[r], pad], axis=0).astype(BF)


def table_kernel(y_ref, ids_f, ids_b, out_f, out_b):
    n = ids_f.shape[1]
    eye = lax.broadcasted_iota(jnp.int32, (n, n), 0) == lax.broadcasted_iota(
        jnp.int32, (n, n), 1
    )
    eye = eye.astype(F32)
    for ids, out in ((ids_f, out_f), (ids_b, out_b)):
        table = slot_table(ids[...], y_ref[0]).astype(F32)
        for d in range(NY):
            out[d] = nt(eye, table[d * CAP : (d + 1) * CAP]).astype(BF)


def held_kernel(v_ref, *refs):
    out, sem = refs[-2:]
    c = pltpu.make_async_copy(v_ref, out, sem)
    c.start()
    c.wait()


def parts_kernel(left, right, out_a, out_b):
    half = out_a.shape[0]
    out_a[...] = left[:half, :]
    out_b[...] = right[half:, :]


def parts_cores_kernel(core_ref, one, two, out_a, out_b):
    half = out_a.shape[0]
    first = core_ref[0] == 0

    @pl.when(first)
    def _():
        out_a[...] = one[:half, :]
        out_b[...] = two[half:, :]

    @pl.when(jnp.logical_not(first))
    def _():
        out_a[...] = two[:half, :]
        out_b[...] = one[half:, :]


def up_kernel(core_ref, r0, r1, r2, r3, token, own, one, two, out):
    rows = jnp.concatenate([r[0 : 2 * CAP, :] for r in (r0, r1, r2, r3)], axis=0)
    n = own.shape[1]
    first = core_ref[0] == 0
    a, b = nn(rows, one[...]), nn(rows, two[...])
    out[:, :n] = nn(rows, own[...]).astype(BF)
    out[:, n : 2 * n] = jnp.where(first, a, b).astype(BF)
    out[:, 2 * n :] = jnp.where(first, b, a).astype(BF)


def up_halves_kernel(r0, r1, r2, r3, wa, wb, out):
    rows = jnp.concatenate([r[0 : 2 * CAP, :] for r in (r0, r1, r2, r3)], axis=0)
    half = wa.shape[0]
    out[...] = (nn(rows[:, :half], wa[...]) + nn(rows[:, half:], wb[...])).astype(BF)


def down_kernel(r0, r1, r2, r3, token, *refs):
    *weights, out = refs
    rows = jnp.concatenate([r[2 * CAP : ROWS, :] for r in (r0, r1, r2, r3)], axis=0)
    at = 0
    for w in weights:
        n = w.shape[0]
        out[:, at : at + n] = nt(rows, w[...]).astype(BF)
        at += n


def pick(v, start, stride):
    return jnp.concatenate(
        [v[i * stride + start : i * stride + start + CAP, :] for i in range(NY)], axis=0
    )


def added(a, b):
    return a.astype(F32) + b.astype(F32)


def activate(pu):
    v = pick(pu, 0, 2 * CAP)
    return (v * jax.nn.sigmoid(v)).astype(BF)


def grad_hidden(pu, pv):
    v = pick(pu, CAP, 2 * CAP)
    g = pick(pv, 0, ROWS - 2 * CAP)
    q = jax.nn.sigmoid(v)
    return (g * (q * (1.0 + v * (1.0 - q)))).astype(BF)


def mid_kernel(core_ref, r0, r1, r2, r3, pu, qu, pv, qv, u0, u1, u2, v0, v1, v2, acc_f, acc_b):
    su = added(pu[...], qu[...])
    act = activate(su)
    hid = grad_hidden(su, added(pv[...], qv[...]))
    first = core_ref[0] == 0
    left, right = hid[:, 256:512].astype(F32), hid[:, 512:].astype(F32)
    hids = (
        hid[:, :256],
        jnp.where(first, left, right).astype(BF),
        jnp.where(first, right, left).astype(BF),
    )
    for c in columns(acc_f.shape[1]):
        rows = [r[:, c].astype(F32) for r in (r0, r1, r2, r3)]
        f = jnp.concatenate([r[:CAP] for r in rows], axis=0)
        b = jnp.concatenate([r[2 * CAP : 3 * CAP] for r in rows], axis=0)
        for i, (u, v) in enumerate(((u0, v0), (u1, v1), (u2, v2))):
            f += nn(act[:, i * 256 : (i + 1) * 256], v[:, c])
            b += nt(hids[i], u[c, :])
        acc_f[:, c] = f
        acc_b[:, c] = b


def last_f_kernel(r0, r1, r2, r3, pu, qu, va, vb, acc, token, out, *outs):
    rows = jnp.concatenate([r[2 * CAP : ROWS, :] for r in (r0, r1, r2, r3)], axis=0)
    out[...] = nt(rows, jnp.concatenate([va[...], vb[...]], axis=0)).astype(BF)
    act = activate(added(pu[...], qu[...]))
    for c in columns(acc.shape[1]):
        t = acc[:, c] + nn(act, jnp.concatenate([va[:, c], vb[:, c]], axis=0))
        for i, o in enumerate(outs):
            o[:, c] = t[i * CAP : (i + 1) * CAP].astype(BF)


def last_b_kernel(pu, qu, pv, qv, ua, ub, acc, token, *outs, parts):
    hid = grad_hidden(added(pu[...], qu[...]), added(pv[...], qv[...]))
    half = ua.shape[0]
    for c in columns(acc.shape[1]):
        pieces = []
        if c.start < half:
            pieces.append(ua[c.start : min(c.stop, half), :])
        if c.stop > half:
            pieces.append(ub[max(c.start, half) - half : c.stop - half, :])
        t = acc[:, c] + nt(hid, jnp.concatenate(pieces, axis=0))
        for i, out in zip(parts, outs):
            out[:, c] = t[i * CAP : (i + 1) * CAP].astype(BF)


def finish_kernel(table, total_f, total_b, row, *refs, stream, group):
    outs, held, sems = refs[:2], refs[2], refs[3]
    copies = []
    for k in (1 - stream, stream):
        total = (total_f, total_b)[k]
        for c in columns(total.shape[1]):
            t = total[:, c]
            if k == stream:
                t += nn(table[group], row[:, c])
            held[k, :, c] = t.astype(held.dtype)
        copies.append(pltpu.make_async_copy(held.at[k], outs[k], sems.at[k]))
        copies[-1].start()
    for c in copies:
        c.wait()


def combine_kernel(table, token, *refs, parts, first):
    *rows, out = refs if first else refs[1:]
    for c in columns(out.shape[1]):
        t = 0.0 if first else refs[0][:, c]
        for d, r in zip(parts, rows):
            t += nn(table[d], r[:, c])
        out[:, c] = t.astype(out.dtype)


def per_device(
    stream_up, routes_up, cotangent_down, saved_down, routes_down, weight_up, weight_down
):
    u_own = weight_up[0, 0]
    v_own = weight_down[0, 0]
    fwd = stream_up[0]
    cot = cotangent_down[0]
    saved = saved_down[0, 0]
    n, width = fwd.shape
    hp = u_own.shape[1]
    ids_up = routes_up.reshape(1, n)
    ids_down = routes_down.reshape(1, n)
    y = (lax.axis_index("expert") // NX).reshape(1)
    core = lax.axis_index("dp").reshape(1)
    mm = 2 * 320 * width * hp

    def parts(left, right, cost):
        half = sds((left.shape[0] // 2, left.shape[1]))
        return call(
            parts_kernel, [half] * 2, cost, 4 * half.shape[0] * half.shape[1], [VM] * 2, left, right
        )

    u_1, u_2 = move_x_cores(u_own, 1), move_x_cores(u_own, -1)
    v_l, v_r = move_x(v_own, 1), move_x(v_own, -1)
    half_u = sds((width // 2, hp))
    to_r, to_l = call(
        parts_cores_kernel,
        [half_u] * 2,
        CU,
        4 * width * hp,
        [SM, VM, VM],
        core,
        u_1,
        u_2,
    )
    to_u = to_r
    u_a, u_b = move_x(to_r, 1), move_x(to_l, -1)
    to_r, to_l = parts(v_l, v_r, 0)
    to_v = to_r
    v_a, v_b = move_x(to_r, 1), move_x(to_l, -1)

    ids_f, ids_b = move_z(ids_up, 1), move_z(ids_down, -1)
    table_f, table_b = call(
        table_kernel, [sds((NY, n, CAP))] * 2, 0, 4 * NY * CAP * n, [SM, VM, VM], y, ids_f, ids_b
    )

    def held(v, cost, *tokens):
        return call(
            held_kernel,
            sds(v.shape),
            cost,
            4 * ROWS * width,
            [ANY] * (1 + len(tokens)),
            v,
            *tokens,
            scratch=[pltpu.SemaphoreType.DMA],
        )

    sent = call(
        dispatch_kernel,
        [sds((ROWS, width))] * NY,
        6 * 160 * 128 * width,
        7 * 128 * width * 2,
        [SM] + [ANY] * 5,
        y,
        ids_up,
        ids_down,
        fwd,
        saved,
        cot,
        scratch=[pltpu.VMEM((1, n), jnp.int32)] * 2
        + [pltpu.VMEM((n, width), BF)] * 3
        + [pltpu.SemaphoreType.DMA((5,))],
    )
    row2 = move_y(sent[2], 2)
    row1 = move_y(held(sent[1], 0, row2, table_f), 1)
    row3 = move_y(held(sent[3], 0, row1, to_u), 3)
    rows = [sent[0], row1, row2, row3]

    pu = call(
        up_kernel,
        sds((2 * CAP * NY, 3 * hp)),
        3 * mm,
        4 << 20,
        [SM] + [VM] * 4 + [ANY] + [VM] * 3,
        core,
        *rows,
        to_v,
        u_own,
        u_1,
        u_2,
    )
    qu = swap(pu)
    pv = call(
        down_kernel,
        sds(((ROWS - 2 * CAP) * NY, 3 * hp)),
        2 * mm,
        4 << 20,
        [VM] * 4 + [ANY] + [VM] * 3,
        *rows,
        pu,
        v_own,
        v_l,
        v_r,
    )
    qv = swap(pv)
    acc_f, acc_b = call(
        mid_kernel,
        [sds((NY * CAP, width), F32)] * 2,
        3 * mm,
        8 << 20,
        [SM] + [VM] * 14,
        core,
        *rows,
        pu,
        qu,
        pv,
        qv,
        u_own,
        u_1,
        u_2,
        v_own,
        v_l,
        v_r,
    )
    pu2 = call(up_halves_kernel, sds((2 * CAP * NY, hp)), CU2, 2 << 20, [VM] * 6, *rows, u_a, u_b)
    qu2 = swap(pu2)
    pv2, *res_f = call(
        last_f_kernel,
        [sds(((ROWS - 2 * CAP) * NY, hp))] + [sds((CAP, width))] * NY,
        mm,
        2 << 20,
        [VM] * 9 + [ANY],
        *rows,
        pu2,
        qu2,
        v_a,
        v_b,
        acc_f,
        acc_b,
    )
    qv2 = swap(pv2)
    res_b = call(
        functools.partial(last_b_kernel, parts=range(NY)),
        [sds((CAP, width))] * NY,
        mm // 2,
        2 << 20,
        [VM] * 7 + [ANY],
        pu2,
        qu2,
        pv2,
        qv2,
        u_a,
        u_b,
        acc_b,
        res_f[0],
    )
    got_f = [move_zy(r, 1, -d) for d, r in enumerate(res_f)]
    got_b = [move_zy(r, -1, -d) for d, r in enumerate(res_b)]

    def combine(table, got, parts, total, token):
        return call(
            functools.partial(combine_kernel, parts=parts, first=total is None),
            sds((n, width), F32),
            2 * CAP * n * width * len(parts),
            8 * n * width,
            [VM, ANY] + [VM] * (len(parts) + (total is not None)),
            table,
            token,
            *(() if total is None else (total,)),
            *[got[d] for d in parts],
        )

    def finish(total_f, total_b, stream, group):
        return call(
            functools.partial(finish_kernel, stream=stream, group=group),
            [sds((n, width))] * 2,
            2 * CAP * n * width,
            12 * n * width,
            [VM] * 4,
            (table_f, table_b)[stream],
            total_f,
            total_b,
            (got_f, got_b)[stream][group],
            scratch=[
                pltpu.VMEM((2, n, width), BF),
                pltpu.SemaphoreType.DMA((2,)),
            ],
            out_specs=[ANY, ANY],
        )

    sum_f = combine(table_f, got_f, (2,), None, table_b)
    sum_b = combine(table_b, got_b, (3,), None, sum_f)
    sum_f = combine(table_f, got_f, (1,), sum_f, sum_b)
    sum_b = combine(table_b, got_b, (0,), sum_b, sum_f)
    sum_f = combine(table_f, got_f, (3,), sum_f, sum_b)
    sum_b = combine(table_b, got_b, (1,), sum_b, sum_f)
    sum_b = combine(table_b, got_b, (2,), sum_b, sum_b)
    out_f, out_b = finish(sum_f, sum_b, 0, 0)
    return (out_f[None], out_b[None])


def solution(mesh):
    return jax.shard_map(
        per_device,
        mesh=mesh,
        in_specs=(
            P("section", "expert", "dp"),
            P("section", None, "expert", None),
            P("section", "expert", "dp"),
            P("section", None, "expert", "dp"),
            P("section", None, "expert", None),
            P("section", "expert", "dp", None),
            P("section", "expert", None, "dp"),
        ),
        out_specs=(P("section", "expert", "dp"), P("section", "expert", "dp")),
        check_vma=False,
    )
```

```python
import functools

import jax
import jax.numpy as jnp
from jax import lax
from jax.experimental import pallas as pl
from jax.experimental.pallas import tpu as pltpu
from jax.sharding import PartitionSpec as P

NX = 4
NY = 4
NZ = 8
CAP = 40
ROWS = 128
BF = jnp.bfloat16
F32 = jnp.float32
VM = pl.BlockSpec(memory_space=pltpu.VMEM)
ANY = pl.BlockSpec(memory_space=pl.ANY)
HBM = pl.BlockSpec(memory_space=pltpu.HBM)
SM = pl.BlockSpec(memory_space=pltpu.SMEM)
CU = 8 * 10**9
CU2 = 6 * 10**9
LIMIT = 24 * 1024 * 1024


def move_x(v, d):
    return lax.ppermute(
        v, "expert", [(y * NX + x, y * NX + (x + d) % NX) for y in range(NY) for x in range(NX)]
    )


def move_y(v, d):
    return lax.ppermute(
        v, "expert", [(y * NX + x, (y + d) % NY * NX + x) for y in range(NY) for x in range(NX)]
    )


def move_z(v, d):
    return lax.ppermute(v, "section", [(z, (z + d) % NZ) for z in range(NZ)])


def move_zy(v, dz, dy):
    n = NX * NY
    pairs = [
        (z * n + y * NX + x, (z + dz) % NZ * n + (y + dy) % NY * NX + x)
        for z in range(NZ)
        for y in range(NY)
        for x in range(NX)
    ]
    return lax.ppermute(v, ("section", "expert"), pairs)


def swap(v):
    return lax.ppermute(v, "dp", [(0, 1), (1, 0)])


def call(kernel, outs, flops, nbytes, in_specs, *args, scratch=(), out_specs=None):
    return pl.pallas_call(
        kernel,
        out_shape=outs,
        scratch_shapes=scratch,
        in_specs=in_specs,
        out_specs=out_specs or jax.tree.map(lambda _: VM, outs),
        compiler_params=pltpu.CompilerParams(vmem_limit_bytes=LIMIT),
        cost_estimate=pl.CostEstimate(flops=flops, bytes_accessed=nbytes, transcendentals=0),
    )(*args)


def sds(shape, dtype=BF):
    return jax.ShapeDtypeStruct(shape, dtype)


def nn(a, b):
    return jnp.dot(a, b, preferred_element_type=F32)


def nt(a, b):
    return lax.dot_general(a, b, (((1,), (1,)), ((), ())), preferred_element_type=F32)


def tn(a, b):
    return lax.dot_general(a, b, (((0,), (0,)), ((), ())), preferred_element_type=F32)


def slot_table(ids, y):
    n = ids.shape[1]
    rel = jnp.bitwise_and(ids - y + NY, NY - 1)
    onehot = (lax.broadcasted_iota(jnp.int32, (8, n), 0) == rel).astype(F32)
    earlier = lax.broadcasted_iota(jnp.int32, (n, n), 0) < lax.broadcasted_iota(
        jnp.int32, (n, n), 1
    )
    before = nn(onehot.astype(BF), earlier.astype(F32).astype(BF))
    rank = jnp.sum(before * onehot, axis=0, keepdims=True).astype(jnp.int32)
    slot = rel * CAP + rank
    table = lax.broadcasted_iota(jnp.int32, (NY * CAP, n), 0) == slot
    return table.astype(F32).astype(BF)


def columns(width, step=256):
    return [slice(c, c + step) for c in range(0, width, step)]


def dispatch_kernel(y_ref, *refs):
    ins, outs, scratch, sems = refs[:5], refs[5:9], refs[9:14], refs[14]
    copies = [pltpu.make_async_copy(i, s, sems.at[k]) for k, (i, s) in enumerate(zip(ins, scratch))]
    for c in copies:
        c.start()
    up, down, fwd, saved, grad = scratch
    y = y_ref[0]
    copies[0].wait()
    copies[1].wait()
    table_up = slot_table(up[...], y)
    table_down = slot_table(down[...], y)
    for c in copies[2:]:
        c.wait()
    for c in columns(fwd.shape[1]):
        f = nn(table_up, fwd[:, c])
        s = nn(table_down, saved[:, c])
        g = nn(table_down, grad[:, c])
        pad = jnp.zeros((ROWS - 3 * CAP, f.shape[1]), F32)
        for rel in range(NY):
            r = slice(rel * CAP, (rel + 1) * CAP)
            outs[rel][:, c] = jnp.concatenate([f[r], s[r], g[r], pad], axis=0).astype(BF)


def table_kernel(y_ref, ids_f, ids_b, out_f, out_b):
    n = ids_f.shape[1]
    eye = lax.broadcasted_iota(jnp.int32, (n, n), 0) == lax.broadcasted_iota(
        jnp.int32, (n, n), 1
    )
    eye = eye.astype(F32)
    for ids, out in ((ids_f, out_f), (ids_b, out_b)):
        table = slot_table(ids[...], y_ref[0]).astype(F32)
        for d in range(NY):
            out[d] = nt(eye, table[d * CAP : (d + 1) * CAP]).astype(BF)


def held_kernel(v_ref, *refs):
    out, sem = refs[-2:]
    c = pltpu.make_async_copy(v_ref, out, sem)
    c.start()
    c.wait()


def parts_kernel(left, right, out_a, out_b):
    half = out_a.shape[0]
    out_a[...] = left[:half, :]
    out_b[...] = right[half:, :]


def up_kernel(r0, r1, r2, r3, token, *refs):
    *weights, out = refs
    rows = jnp.concatenate([r[0 : 2 * CAP, :] for r in (r0, r1, r2, r3)], axis=0)
    for i, w in enumerate(weights):
        out[:, i * 256 : (i + 1) * 256] = nn(rows, w[...]).astype(BF)


def up_halves_kernel(r0, r1, r2, r3, wa, wb, out):
    rows = jnp.concatenate([r[0 : 2 * CAP, :] for r in (r0, r1, r2, r3)], axis=0)
    half = wa.shape[0]
    out[...] = (nn(rows[:, :half], wa[...]) + nn(rows[:, half:], wb[...])).astype(BF)


def down_kernel(r0, r1, r2, r3, token, *refs):
    *weights, out = refs
    rows = jnp.concatenate([r[2 * CAP : ROWS, :] for r in (r0, r1, r2, r3)], axis=0)
    at = 0
    for w in weights:
        n = w.shape[0]
        out[:, at : at + n] = nt(rows, w[...]).astype(BF)
        at += n


def pick(v, start, stride):
    return jnp.concatenate(
        [v[i * stride + start : i * stride + start + CAP, :] for i in range(NY)], axis=0
    )


def added(a, b):
    return a.astype(F32) + b.astype(F32)


def activate(pu):
    v = pick(pu, 0, 2 * CAP)
    return (v * jax.nn.sigmoid(v)).astype(BF)


def grad_hidden(pu, pv):
    v = pick(pu, CAP, 2 * CAP)
    g = pick(pv, 0, ROWS - 2 * CAP)
    q = jax.nn.sigmoid(v)
    return (g * (q * (1.0 + v * (1.0 - q)))).astype(BF)


def mid_kernel(r0, r1, r2, r3, pu, qu, pv, qv, u0, u1, u2, v0, v1, v2, acc_f, acc_b):
    su = added(pu[...], qu[...])
    act = activate(su)
    hid = grad_hidden(su, added(pv[...], qv[...]))
    for c in columns(acc_f.shape[1]):
        rows = [r[:, c].astype(F32) for r in (r0, r1, r2, r3)]
        f = jnp.concatenate([r[:CAP] for r in rows], axis=0)
        b = jnp.concatenate([r[2 * CAP : 3 * CAP] for r in rows], axis=0)
        for i, (u, v) in enumerate(((u0, v0), (u1, v1), (u2, v2))):
            f += nn(act[:, i * 256 : (i + 1) * 256], v[:, c])
            b += nt(hid[:, i * 256 : (i + 1) * 256], u[c, :])
        acc_f[:, c] = f
        acc_b[:, c] = b


def last_f_kernel(r0, r1, r2, r3, pu, qu, va, vb, acc, token, out, *outs):
    rows = jnp.concatenate([r[2 * CAP : ROWS, :] for r in (r0, r1, r2, r3)], axis=0)
    out[...] = nt(rows, jnp.concatenate([va[...], vb[...]], axis=0)).astype(BF)
    act = activate(added(pu[...], qu[...]))
    for c in columns(acc.shape[1]):
        t = acc[:, c] + nn(act, jnp.concatenate([va[:, c], vb[:, c]], axis=0))
        for i, o in enumerate(outs):
            o[:, c] = t[i * CAP : (i + 1) * CAP].astype(BF)


def last_b_kernel(pu, qu, pv, qv, ua, ub, acc, token, *outs, parts):
    hid = grad_hidden(added(pu[...], qu[...]), added(pv[...], qv[...]))
    half = ua.shape[0]
    for c in columns(acc.shape[1]):
        pieces = []
        if c.start < half:
            pieces.append(ua[c.start : min(c.stop, half), :])
        if c.stop > half:
            pieces.append(ub[max(c.start, half) - half : c.stop - half, :])
        t = acc[:, c] + nt(hid, jnp.concatenate(pieces, axis=0))
        for i, out in zip(parts, outs):
            out[:, c] = t[i * CAP : (i + 1) * CAP].astype(BF)


def finish_kernel(table, total_f, total_b, row, *refs, stream, group):
    outs, held, sems = refs[:2], refs[2], refs[3]
    copies = []
    for k in (1 - stream, stream):
        total = (total_f, total_b)[k]
        for c in columns(total.shape[1]):
            t = total[:, c]
            if k == stream:
                t += nn(table[group], row[:, c])
            held[k, :, c] = t.astype(held.dtype)
        copies.append(pltpu.make_async_copy(held.at[k], outs[k], sems.at[k]))
        copies[-1].start()
    for c in copies:
        c.wait()


def combine_kernel(table, token, *refs, parts, first):
    *rows, out = refs if first else refs[1:]
    for c in columns(out.shape[1]):
        t = 0.0 if first else refs[0][:, c]
        for d, r in zip(parts, rows):
            t += nn(table[d], r[:, c])
        out[:, c] = t.astype(out.dtype)


def per_device(
    stream_up, routes_up, cotangent_down, saved_down, routes_down, weight_up, weight_down
):
    u_own = weight_up[0, 0]
    v_own = weight_down[0, 0]
    fwd = stream_up[0]
    cot = cotangent_down[0]
    saved = saved_down[0, 0]
    n, width = fwd.shape
    hp = u_own.shape[1]
    ids_up = routes_up.reshape(1, n)
    ids_down = routes_down.reshape(1, n)
    y = (lax.axis_index("expert") // NX).reshape(1)
    mm = 2 * 320 * width * hp

    def parts(left, right, cost):
        half = sds((left.shape[0] // 2, left.shape[1]))
        return call(
            parts_kernel, [half] * 2, cost, 4 * half.shape[0] * half.shape[1], [VM] * 2, left, right
        )

    u_l, u_r = move_x(u_own, 1), move_x(u_own, -1)
    v_l, v_r = move_x(v_own, 1), move_x(v_own, -1)
    to_r, to_l = parts(u_l, u_r, CU)
    to_u = to_r
    u_a, u_b = move_x(to_r, 1), move_x(to_l, -1)
    to_r, to_l = parts(v_l, v_r, 0)
    to_v = to_r
    v_a, v_b = move_x(to_r, 1), move_x(to_l, -1)

    ids_f, ids_b = move_z(ids_up, 1), move_z(ids_down, -1)
    table_f, table_b = call(
        table_kernel, [sds((NY, n, CAP))] * 2, 0, 4 * NY * CAP * n, [SM, VM, VM], y, ids_f, ids_b
    )

    def held(v, cost, *tokens):
        return call(
            held_kernel,
            sds(v.shape),
            cost,
            4 * ROWS * width,
            [ANY] * (1 + len(tokens)),
            v,
            *tokens,
            scratch=[pltpu.SemaphoreType.DMA],
        )

    sent = call(
        dispatch_kernel,
        [sds((ROWS, width))] * NY,
        6 * 160 * 128 * width,
        7 * 128 * width * 2,
        [SM] + [ANY] * 5,
        y,
        ids_up,
        ids_down,
        fwd,
        saved,
        cot,
        scratch=[pltpu.VMEM((1, n), jnp.int32)] * 2
        + [pltpu.VMEM((n, width), BF)] * 3
        + [pltpu.SemaphoreType.DMA((5,))],
    )
    row2 = move_y(sent[2], 2)
    row1 = move_y(held(sent[1], 0, row2, table_f), 1)
    row3 = move_y(held(sent[3], 0, row1, to_u), 3)
    rows = [sent[0], row1, row2, row3]

    pu = call(
        up_kernel,
        sds((2 * CAP * NY, 3 * hp)),
        3 * mm,
        4 << 20,
        [VM] * 4 + [ANY] + [VM] * 3,
        *rows,
        to_v,
        u_own,
        u_l,
        u_r,
    )
    qu = swap(pu)
    pv = call(
        down_kernel,
        sds(((ROWS - 2 * CAP) * NY, 3 * hp)),
        2 * mm,
        4 << 20,
        [VM] * 4 + [ANY] + [VM] * 3,
        *rows,
        pu,
        v_own,
        v_l,
        v_r,
    )
    qv = swap(pv)
    acc_f, acc_b = call(
        mid_kernel,
        [sds((NY * CAP, width), F32)] * 2,
        3 * mm,
        8 << 20,
        [VM] * 14,
        *rows,
        pu,
        qu,
        pv,
        qv,
        u_own,
        u_l,
        u_r,
        v_own,
        v_l,
        v_r,
    )
    pu2 = call(up_halves_kernel, sds((2 * CAP * NY, hp)), CU2, 2 << 20, [VM] * 6, *rows, u_a, u_b)
    qu2 = swap(pu2)
    pv2, *res_f = call(
        last_f_kernel,
        [sds(((ROWS - 2 * CAP) * NY, hp))] + [sds((CAP, width))] * NY,
        mm,
        2 << 20,
        [VM] * 9 + [ANY],
        *rows,
        pu2,
        qu2,
        v_a,
        v_b,
        acc_f,
        acc_b,
    )
    qv2 = swap(pv2)
    res_b = call(
        functools.partial(last_b_kernel, parts=range(NY)),
        [sds((CAP, width))] * NY,
        mm // 2,
        2 << 20,
        [VM] * 7 + [ANY],
        pu2,
        qu2,
        pv2,
        qv2,
        u_a,
        u_b,
        acc_b,
        res_f[0],
    )
    got_f = [move_zy(r, 1, -d) for d, r in enumerate(res_f)]
    got_b = [move_zy(r, -1, -d) for d, r in enumerate(res_b)]

    def combine(table, got, parts, total, token):
        return call(
            functools.partial(combine_kernel, parts=parts, first=total is None),
            sds((n, width), F32),
            2 * CAP * n * width * len(parts),
            8 * n * width,
            [VM, ANY] + [VM] * (len(parts) + (total is not None)),
            table,
            token,
            *(() if total is None else (total,)),
            *[got[d] for d in parts],
        )

    def finish(total_f, total_b, stream, group):
        return call(
            functools.partial(finish_kernel, stream=stream, group=group),
            [sds((n, width))] * 2,
            2 * CAP * n * width,
            12 * n * width,
            [VM] * 4,
            (table_f, table_b)[stream],
            total_f,
            total_b,
            (got_f, got_b)[stream][group],
            scratch=[
                pltpu.VMEM((2, n, width), BF),
                pltpu.SemaphoreType.DMA((2,)),
            ],
            out_specs=[ANY, ANY],
        )

    sum_f = combine(table_f, got_f, (3,), None, table_b)
    sum_b = combine(table_b, got_b, (1,), None, sum_f)
    sum_f = combine(table_f, got_f, (0,), sum_f, sum_b)
    sum_b = combine(table_b, got_b, (0,), sum_b, sum_f)
    sum_f = combine(table_f, got_f, (2,), sum_f, sum_b)
    sum_f = combine(table_f, got_f, (1,), sum_f, sum_f)
    sum_b = combine(table_b, got_b, (3,), sum_b, sum_f)
    out_f, out_b = finish(sum_f, sum_b, 1, 2)
    return (out_f[None], out_b[None])


def solution(mesh):
    return jax.shard_map(
        per_device,
        mesh=mesh,
        in_specs=(
            P("section", "expert", "dp"),
            P("section", None, "expert", None),
            P("section", "expert", "dp"),
            P("section", None, "expert", "dp"),
            P("section", None, "expert", None),
            P("section", "expert", "dp", None),
            P("section", "expert", None, "dp"),
        ),
        out_specs=(P("section", "expert", "dp"), P("section", "expert", "dp")),
        check_vma=False,
    )
```
